128 devices in a mesh: pipe: 2 (over y_lo), tensor: 2 (over y_hi), ctx: 32 (over x, z, core).
Axes of the slice: x: 4, y: 4 (y_hi: 2, y_lo: 2; y = y_hi * 2 + y_lo), z: 4, core: 2. Of those that a mesh axis runs over, the one named last changes fastest.
Arguments:
- inputs: bfloat16 [2, 4096, 768], P(None, 'ctx', 'tensor'), may hold values from -6 to 6
- cotangent: bfloat16 [2, 4096, 768], P(None, 'ctx', 'tensor'), may hold values from -6 to 6
- ln_gain: bfloat16 [2, 2, 768], P('pipe'), may hold values from 0.5 to 1.5
- ln_bias: bfloat16 [2, 2, 768], P('pipe'), may hold values from -1.5 to 1.5
- qkv_weight: bfloat16 [2, 3, 768, 768], P('pipe', None, None, 'tensor'), may hold values from -0.21875 to 0.21875
- qkv_bias: bfloat16 [2, 3, 768], P('pipe', None, 'tensor'), may hold values from -1.5 to 1.5
- out_weight: bfloat16 [2, 768, 768], P('pipe', 'tensor'), may hold values from -1.5 to 1.5
- out_bias: bfloat16 [2, 768], P('pipe', 'tensor'), may hold values from -1.5 to 1.5
- fc_in_weight: bfloat16 [2, 768, 3072], P('pipe', None, 'tensor'), may hold values from -0.21875 to 0.21875
- fc_in_bias: bfloat16 [2, 3072], P('pipe', 'tensor'), may hold values from -2.5 to 2.5
- fc_out_weight: bfloat16 [2, 3072, 768], P('pipe', 'tensor'), may hold values from -0.109375 to 0.109375
Outputs:
- boundary: bfloat16 [2, 2, 4096, 768], P('pipe', None, 'ctx', 'tensor')
- ln_gain_grad: float32 [2, 2, 768], P('pipe', None, 'tensor')
- ln_bias_grad: float32 [2, 2, 768], P('pipe', None, 'tensor')
- qkv_weight_grad: float32 [2, 3, 768, 768], P('pipe', None, None, 'tensor')
- qkv_bias_grad: float32 [2, 3, 768], P('pipe', None, 'tensor')
- out_weight_grad: float32 [2, 768, 768], P('pipe', 'tensor')
- out_bias_grad: float32 [2, 768], P('pipe', 'tensor')
- fc_in_weight_grad: float32 [2, 768, 3072], P('pipe', None, 'tensor')
- fc_in_bias_grad: float32 [2, 3072], P('pipe', 'tensor')
- fc_out_weight_grad: float32 [2, 3072, 768], P('pipe', 'tensor')
The draws below stay inside these ranges and needn't reach their ends.
All inputs are finite; a program needn't handle non-finite values.
Results may differ from the reference program's by a relative error of at most 0.02.
Values may be sent and summed in bfloat16 or wider, within the bound.
A program may use at most 192 MiB of HBM per device.

```python
import jax
import jax.numpy as jnp
from jax import lax

D = 768
HD = 64
FF = 3072
MICRO = 2
SECTIONS = 2
SEQ = 4096


def steps_of(stream_key, dims, cuts, low, top_value):
    level, own = 1.0, jax.random.fold_in(stream_key, 6)
    for position, blocks in cuts:
        heights = jnp.exp(jax.random.uniform(jax.random.fold_in(own, position), (blocks,), jnp.float32, low / len(cuts), top_value / len(cuts)))
        level = level * jnp.repeat(heights, dims[position] // blocks).reshape([-1 if axis == position else 1 for axis in range(len(dims))])
    return level


def gaussian(key, shape, scale, most, cuts=(), kind=jnp.bfloat16):
    result = scale * jax.random.normal(key, shape, jnp.float32)
    if cuts:
        result = result * steps_of(key, shape, cuts, -0.22, 0.18)
    return jnp.clip(result, -most, most).astype(kind)


def setup_inputs(seed: int = 0) -> dict:
    streams_of = jax.random.split(jax.random.key(seed), 12)
    return {
        "inputs": gaussian(streams_of[0], (MICRO, SEQ, D), 1.0, 6.0, ((1, 32), (2, 2))),
        "cotangent": gaussian(streams_of[1], (MICRO, SEQ, D), 1.0, 6.0, ((1, 32), (2, 2))),
        "ln_gain": jnp.clip(1.0 + 0.1 * jax.random.normal(streams_of[2], (SECTIONS, 2, D), jnp.float32), 0.5, 1.5).astype(jnp.bfloat16),
        "ln_bias": gaussian(streams_of[3], (SECTIONS, 2, D), 0.3, 1.5, ((0, 2),)),
        "qkv_weight": gaussian(streams_of[4], (SECTIONS, 3, D, D), D ** -0.5, 0.21875, ((0, 2), (3, 2))),
        "qkv_bias": gaussian(streams_of[5], (SECTIONS, 3, D), 0.3, 1.5, ((0, 2), (2, 2))),
        "out_weight": gaussian(streams_of[6], (SECTIONS, D, D), 16 ** -0.5, 1.5, ((0, 2), (1, 2))),
        "out_bias": gaussian(streams_of[7], (SECTIONS, D), 0.3, 1.5, ((0, 2), (1, 2))),
        "fc_in_weight": gaussian(streams_of[8], (SECTIONS, D, FF), D ** -0.5, 0.21875, ((0, 2), (2, 2))),
        "fc_in_bias": gaussian(streams_of[9], (SECTIONS, FF), 0.5, 2.5, ((0, 2), (1, 2))),
        "fc_out_weight": gaussian(streams_of[10], (SECTIONS, FF, D), FF ** -0.5, 0.109375, ((0, 2), (1, 2))),
    }


@jax.custom_vjp
def low(v):
    return lax.optimization_barrier(v.astype(jnp.bfloat16)).astype(jnp.float32)

@jax.custom_vjp
def low_back(v):
    return v

def low_keep(v):
    return (low(v), None)

def low_pass(kept, grad):
    return (grad,)

def back_keep(v):
    return (v, None)

def back_low(kept, grad):
    return (low(grad),)
low.defvjp(low_keep, low_pass)
low_back.defvjp(back_keep, back_low)
norm_eps = 1e-05
masked_score = -1e+30

def normalize(values):
    centered = values - lax.optimization_barrier(jnp.mean(values, axis=-1, keepdims=True))
    variance = lax.optimization_barrier(jnp.mean(centered * centered, axis=-1, keepdims=True))
    scale = lax.rsqrt(variance + norm_eps)
    return (centered * scale, scale)

def rotate(values, positions):
    rows = values.shape[0]
    split = values.reshape(rows, -1, HD)
    turned_dims = HD // 4
    half = turned_dims // 2
    freqs = 10000.0 ** (-2.0 * jnp.arange(half, dtype=jnp.float32) / turned_dims)
    angles = positions.astype(jnp.float32)[:, None] * freqs[None, :]
    cosine = jnp.cos(angles)[:, None, :]
    sine = jnp.sin(angles)[:, None, :]
    lower = split[:, :, :half]
    upper = split[:, :, half:turned_dims]
    turned = jnp.concatenate([lower * cosine - upper * sine, upper * cosine + lower * sine, split[:, :, turned_dims:]], axis=-1)
    return turned.reshape(rows, -1)

def attention(queries, keys, values):
    total = keys.shape[0]
    block = min(512, total)
    highest = lax.Precision.HIGHEST
    key_heads = keys.reshape(total, -1, HD)
    value_heads = values.reshape(total, -1, HD)
    query_blocks = queries.reshape(total // block, block, -1, HD)
    key_pos = jnp.arange(total, dtype=jnp.int32)

    def one_block(item):
        query_block, start = item
        raw = low_back(jnp.einsum('chd,shd->hcs', query_block, key_heads, precision=highest))
        query_pos = start + jnp.arange(block, dtype=jnp.int32)
        allowed = key_pos[None, None, :] <= query_pos[None, :, None]
        scores = jnp.where(allowed, raw * HD ** (-0.5), masked_score)
        top = lax.optimization_barrier(jnp.max(scores, axis=-1, keepdims=True))
        weights_exp = jnp.exp(scores - top)
        probs = weights_exp / lax.optimization_barrier(jnp.sum(weights_exp, axis=-1, keepdims=True))
        return jnp.einsum('hcs,shd->chd', low(probs), value_heads, precision=highest)
    starts = jnp.arange(total // block, dtype=jnp.int32) * block
    blocks_out = lax.map(jax.checkpoint(one_block), (query_blocks, starts))
    return blocks_out.reshape(total, -1)

def layer(x, gain, shift, qkv_w, qkv_b, out_w, out_b, in_w, in_b, down_w):
    highest = lax.Precision.HIGHEST
    normed, _ = normalize(x)
    first = low(normed * gain[0] + shift[0])
    second = low(normed * gain[1] + shift[1])
    pre_q = low_back(jnp.dot(first, qkv_w[0], precision=highest) + qkv_b[0])
    pre_k = low_back(jnp.dot(first, qkv_w[1], precision=highest) + qkv_b[1])
    pre_v = low_back(jnp.dot(first, qkv_w[2], precision=highest) + qkv_b[2])
    positions = jnp.arange(x.shape[0], dtype=jnp.int32)
    queries = low(rotate(pre_q, positions))
    keys = low(rotate(pre_k, positions))
    values = low(pre_v)
    attn = low_back(low(attention(queries, keys, values)))
    inner = low_back(jnp.dot(second, in_w, precision=highest) + in_b)
    act = low(jax.nn.gelu(inner, approximate=False))
    return x + jnp.dot(attn, out_w, precision=highest) + jnp.dot(act, down_w, precision=highest) + out_b

def reference(inputs, cotangent, ln_gain, ln_bias, qkv_weight, qkv_bias, out_weight, out_bias, fc_in_weight, fc_in_bias, fc_out_weight):
    params = tuple((a.astype(jnp.float32) for a in (ln_gain, ln_bias, qkv_weight, qkv_bias, out_weight, out_bias, fc_in_weight, fc_in_bias, fc_out_weight)))

    def run(pars, x):
        middle = low_back(low(layer(x, *[p[0] for p in pars])))
        return layer(middle, *[p[1] for p in pars])

    def step(acc, item):
        x, grad_top = item
        top, back = jax.vjp(run, params, x.astype(jnp.float32))
        grad_pars, grad_x = back(grad_top.astype(jnp.float32))
        acc = tuple((a + g for a, g in zip(acc, grad_pars)))
        return (acc, (grad_x.astype(jnp.bfloat16), top.astype(jnp.bfloat16)))
    zeros = tuple((jnp.zeros_like(p) for p in params))
    acc, (grad_inputs, tops) = lax.scan(step, zeros, (inputs, cotangent))
    boundary = jnp.stack([grad_inputs, tops])
    return (boundary, acc[0], acc[1], acc[2], acc[3], acc[4], acc[5], acc[6], acc[7], acc[8])
```

```python
import functools

import jax
import jax.numpy as jnp
from jax import lax
from jax.experimental import pallas as pl
from jax.experimental.pallas import tpu as pltpu
from jax.sharding import PartitionSpec as P


D = 768
HD = 64
F32 = jnp.float32
BF = jnp.bfloat16
MESH = pl.DeviceIdType.MESH
EPS = 1e-05
CHIPS = 16
ROWS = 256
PIECE = 144
SLAB = CHIPS * PIECE
KV0, Q0, O0, I0, U0 = 0, 384, 576, 768, 1536
BLOCKS = ((1, 0), (2, 0), (2, 1), (1, 1), (1, 2), (2, 2), (0, 0), (0, 1), (0, 2))
NN = (((1,), (0,)), ((), ()))
NT = (((1,), (1,)), ((), ()))
TN = (((0,), (0,)), ((), ()))


def dot(a, b, dims=NN):
    return lax.dot_general(a, b, dims, preferred_element_type=F32)


class Place:
    def __init__(self):
        self.pipe = lax.axis_index("pipe")
        self.tensor = lax.axis_index("tensor")
        ctx = lax.axis_index("ctx")
        self.core = lax.rem(ctx, 2)
        self.chip = ctx // 2
        self.x = self.chip // 4
        self.z = lax.rem(self.chip, 4)

    def slot(self, dx, dz):
        return lax.rem(self.x + (dx + 4), 4) * 4 + lax.rem(self.z + (dz + 4), 4)

    def at(self, dx, dz):
        return (self.pipe, self.tensor, self.slot(dx, dz) * 2 + self.core)

    def mate(self, r):
        t = lax.rem(self.tensor + r // 2, 2)
        c = lax.rem(self.core + r % 2, 2)
        return t, c, (self.pipe, t, self.chip * 2 + c)

    def partner(self):
        return (1 - self.pipe, self.tensor, self.chip * 2 + self.core)

    def greet(self, mates=(), partner=False, far=False):
        bar = pltpu.get_barrier_semaphore()
        targets = [self.at(1, 0), self.at(-1, 0), self.at(0, 1), self.at(0, -1)]
        if far:
            targets += [self.at(2, 0), self.at(0, 2)]
        targets += [self.mate(r)[2] for r in mates]
        if partner:
            targets.append(self.partner())
        for target in targets:
            pl.semaphore_signal(bar, inc=1, device_id=target, device_id_type=MESH)
        pl.semaphore_wait(bar, len(targets))


class Links:
    def __init__(self, send_sems, recv_sems):
        self.send_sems, self.recv_sems = send_sems, recv_sems
        self.ids, self.sent = {}, []

    def desc(self, key, src, dst, device):
        i = self.ids.setdefault(key, len(self.ids))
        return pltpu.make_async_remote_copy(
            src_ref=src,
            dst_ref=dst,
            send_sem=self.send_sems.at[i],
            recv_sem=self.recv_sems.at[i],
            device_id=device,
            device_id_type=MESH,
        )

    def send(self, key, copy):
        self.desc(key, *copy()).start()
        self.sent.append((key, copy))

    def arrived(self, key, dst, device):
        self.desc(key, dst, dst, device).wait_recv()

    def finish(self):
        for key, copy in self.sent:
            self.desc(key, *copy()).wait_send()


def kv_view(h, part):
    start, size = {"all": (0, 128), 0: (0, 64), 1: (64, 64)}[part]
    return (pl.ds(h * 128 + start, size), pl.ds(0, 384))


def slab_view(h, part):
    cut = (80, 64)[h]
    start, size = {"all": (0, PIECE), 0: (0, cut), 1: (cut, PIECE - cut)}[part]
    return (pl.ds(start, size), pl.ds(h * 384, 384))


class Gather:
    def __init__(self, place, links, buf, view, tag=""):
        self.place, self.links, self.buf, self.view, self.tag = place, links, buf, view, tag

    def ref(self, du, dv, h, part):
        slot = self.place.slot(du, dv) if h == 0 else self.place.slot(dv, du)
        return self.buf.at[(slot,) + self.view(h, part)]

    def dev(self, along_u, step, h):
        return self.place.at(step, 0) if along_u == (h == 0) else self.place.at(0, step)

    def snd(self, h, along_u, step, du, dv, part):
        key = (self.tag, h, along_u, step, du - (step if along_u else 0), dv - (0 if along_u else step), part)
        ref = lambda: self.ref(du, dv, h, part)
        self.links.send(key, lambda: (ref(), ref(), self.dev(along_u, step, h)))

    def rcv(self, h, along_u, step, du, dv, part):
        key = (self.tag, h, along_u, step, du, dv, part)
        self.links.arrived(key, self.ref(du, dv, h, part), self.dev(along_u, step, h))

    def begin(self):
        for along_u in (True, False):
            for h in (0, 1):
                for step in (1, -1):
                    self.snd(h, along_u, step, 0, 0, "all")

    def first(self):
        for h in (0, 1):
            for step, part in ((1, 0), (-1, 1)):
                self.rcv(h, True, step, -step, 0, "all")
                self.snd(h, True, step, -step, 0, part)
                for s in (1, -1):
                    self.snd(h, False, s, -step, 0, "all")

    def second(self):
        for h in (0, 1):
            for step, part in ((1, 0), (-1, 1)):
                self.rcv(h, True, step, -2 * step, 0, part)
            for s in (1, -1):
                self.snd(h, False, s, 2, 0, "all")

    def third(self, du):
        for h in (0, 1):
            for step, part in ((1, 0), (-1, 1)):
                self.rcv(h, False, step, du, -step, "all")
                self.snd(h, False, step, du, -step, part)

    def fourth(self, du):
        for h in (0, 1):
            for step, part in ((1, 0), (-1, 1)):
                self.rcv(h, False, step, du, -2 * step, part)

    def run(self, done=lambda a, b: None):
        self.begin()
        done(0, 0)
        self.first()
        self.second()
        for stage, du, slots in (
            (self.third, 0, ORDER_F[0:4]),
            (self.third, -1, ORDER_F[4:5]),
            (self.third, 1, ORDER_F[5:8]),
            (self.third, 2, ()),
            (self.fourth, 0, ORDER_F[8:10]),
            (self.fourth, -1, ORDER_F[10:12]),
            (self.fourth, 1, ORDER_F[12:14]),
            (self.fourth, 2, ORDER_F[14:15]),
        ):
            stage(du)
            for a, b in slots:
                done(a, b)


class Scatter:
    def __init__(self, place, links, buf, view, r1, r2, u1, u2, tag=""):
        self.place, self.links, self.buf, self.view = place, links, buf, view
        self.r1, self.r2, self.u1, self.u2, self.tag = r1, r2, u1, u2, tag

    def ref(self, du, dv, h, part):
        slot = self.place.slot(du, dv) if h == 0 else self.place.slot(dv, du)
        return self.buf.at[(slot,) + self.view(h, part)]

    def dev(self, along_u, step, h):
        return self.place.at(step, 0) if along_u == (h == 0) else self.place.at(0, step)

    def size(self, h, part):
        return pl.ds(0, self.view(h, part)[0].size)

    def land(self, stage, h, step, du):
        d, e = (step + 1) // 2, (du + 4) % 4
        part = (1 - d) if stage in ("v1", "u1") else "all"
        rows = self.size(h, part)
        return {
            "v1": lambda: self.r1.at[h, d, e, rows],
            "v2": lambda: self.r2.at[h, d, e, rows],
            "u1": lambda: self.u1.at[h, d, rows],
            "u2": lambda: self.u2.at[h, d, rows],
        }[stage]()

    def snd(self, stage, h, step, du, src):
        key = (self.tag, stage, h, step, du)
        device = lambda: self.dev(stage[0] == "u", step, h)
        self.links.send(key, lambda: (src(), self.land(stage, h, step, du), device()))

    def rcv(self, stage, h, step, du):
        ref = self.land(stage, h, step, du)
        self.links.arrived((self.tag, stage, h, step, du), ref, self.dev(stage[0] == "u", step, h))
        return ref

    def v1(self, h, step, du):
        self.snd("v1", h, step, du, lambda: self.ref(du, 2, h, (1 - step) // 2))

    def v2(self, h, step, du):
        got = self.rcv("v1", h, step, du)
        mine = self.ref(du, step, h, (1 - step) // 2)
        mine[...] = (mine[...].astype(F32) + got[...].astype(F32)).astype(BF)
        self.snd("v2", h, step, du, lambda: self.ref(du, step, h, "all"))

    def vsum(self, h, du):
        one, two = self.rcv("v2", h, 1, du), self.rcv("v2", h, -1, du)
        mine = self.ref(du, 0, h, "all")
        mine[...] = (mine[...].astype(F32) + one[...].astype(F32) + two[...].astype(F32)).astype(BF)

    def u1s(self, h):
        for step in (1, -1):
            self.snd("u1", h, step, 0, lambda step=step: self.ref(2, 0, h, (1 - step) // 2))

    def u2s(self, h, step):
        got = self.rcv("u1", h, step, 0)
        mine = self.ref(step, 0, h, (1 - step) // 2)
        mine[...] = (mine[...].astype(F32) + got[...].astype(F32)).astype(BF)
        self.snd("u2", h, step, 0, lambda: self.ref(step, 0, h, "all"))

    def last(self, h):
        one, two = self.rcv("u2", h, 1, 0), self.rcv("u2", h, -1, 0)
        mine = self.ref(0, 0, h, "all")
        return mine[...].astype(F32) + one[...].astype(F32) + two[...].astype(F32)

    def tail_one(self):
        for h in (0, 1):
            self.vsum(h, 2)
            self.u1s(h)

    def tail_two(self):
        for h in (0, 1):
            for step in (1, -1):
                self.vsum(h, step)
                self.u2s(h, step)

    def tail_three(self):
        for h in (0, 1):
            self.vsum(h, 0)


def pick(n, values):
    out = 0
    for j, v in enumerate(values):
        out = out + (n == j).astype(jnp.int32) * v
    return out


def mates_gather(place, links, own, full, tag):
    rows = pl.ds(pl.multiple_of(place.core * 128, 128), 128)
    for r in (1, 2, 3):
        device = place.mate(r)[2]
        links.send((tag, r), lambda device=device: (own, full.at[place.tensor, rows], device))
    full[place.tensor, rows] = own[...]


def mates_gathered(place, links, full, tag):
    for r in (1, 2, 3):
        t, c, device = place.mate(r)
        links.arrived((tag, r), full.at[t, pl.ds(pl.multiple_of(c * 128, 128), 128)], device)


def mates_scatter(place, links, part, rounded, landing, tag):
    rounded[...] = part[...].astype(BF)
    for r in (1, 2, 3):
        t, c, device = place.mate(r)
        src = rounded.at[t, pl.ds(pl.multiple_of(c * 128, 128), 128)]
        links.send((tag, r), lambda r=r, src=src, device=device: (src, landing.at[r - 1], device))


def mates_scattered(place, links, part, landing, tag):
    total = part[place.tensor, pl.ds(pl.multiple_of(place.core * 128, 128), 128)]
    for r in (1, 2, 3):
        links.arrived((tag, r), landing.at[r - 1], place.mate(r)[2])
        total = total + landing[r - 1].astype(F32)
    return total


def normalize(values):
    centered = values - jnp.mean(values, axis=-1, keepdims=True)
    variance = jnp.mean(centered * centered, axis=-1, keepdims=True)
    scale = lax.rsqrt(variance + EPS)
    return centered * scale, scale


def lane_mask(lower, shape=(ROWS, 128)):
    lane = lax.broadcasted_iota(jnp.int32, shape, 1)
    return lane < 64 if lower else lane >= 64


def turn(values, tab, lower, upper, sign=1.0):
    cosine, plus, minus = tab[0], tab[1], tab[2]
    turned = (
        values * cosine
        + sign * (pltpu.roll(values, 8, 1) * plus + pltpu.roll(values, 120, 1) * minus)
    )
    if lower and upper:
        return turned
    return jnp.where(lane_mask(lower), turned, values)


def weights_kernel(
    qkv, out, fc_in, fc_out, gain, shift, qkv_b, in_b, out_b, mine, theirs, all_small,
    own, buf, raw, turned, small, got_small, send_sems, recv_sems, local,
):
    place = Place()
    links = Links(send_sems, recv_sems)
    core = place.core
    loads = [pltpu.make_async_copy(qkv, raw, local.at[0])]
    for i, block in enumerate((1, 0, 2)):
        rows = pl.ds(pl.multiple_of(core * 192 + block * 64, 64), 64)
        loads.append(pltpu.make_async_copy(out.at[rows], own.at[pl.ds(O0 + i * 64, 64)], local.at[1 + i]))
    half = pl.ds(pl.multiple_of(core * 768, 768), 768)
    loads.append(pltpu.make_async_copy(fc_in.at[:, half], own.at[pl.ds(I0, 768)], local.at[4]))
    loads.append(pltpu.make_async_copy(fc_out.at[half], own.at[pl.ds(U0, 768)], local.at[5]))
    for load in loads:
        load.start()
    place.greet(partner=True)
    small[...] = jnp.zeros_like(small)
    small[0:2] = gain[...].astype(F32)
    small[2:4] = shift[...].astype(F32)
    bias = qkv_b[...].astype(F32)
    bias = jnp.where(core == 0, bias[:, 0:192], bias[:, 192:384])
    pieces = [bias[j : j + 1, h * 64 : h * 64 + 64] for j, h in BLOCKS]
    small[4:5, 0:576] = jnp.concatenate(pieces, axis=1)
    wide = in_b[...].astype(F32)
    small[5:6] = jnp.where(core == 0, wide[:, 0:768], wide[:, 768:1536])
    small[6:7, 0:384] = out_b[...].astype(F32)
    rounded = small[...].astype(BF)
    all_small[place.pipe] = rounded
    loads[0].wait()
    for j in range(3):
        turned[...] = raw[j].T
        for i, (k, h) in enumerate(BLOCKS):
            if k == j:
                own[i * 64 : i * 64 + 64, :] = turned[pl.ds(pl.multiple_of(core * 192 + h * 64, 64), 64), :]
    for load in loads[1:]:
        load.wait()
    device = place.partner()
    piece = pl.ds(pl.multiple_of(place.chip * PIECE, PIECE), PIECE)
    links.send("slab", lambda: (own.at[piece], buf.at[place.chip], device))
    got_small[0] = rounded
    links.send("small", lambda: (got_small.at[0], got_small.at[1], device))
    keep = pltpu.make_async_copy(own, mine, local.at[6])
    keep.start()
    links.arrived("slab", buf.at[place.chip], device)
    Gather(place, links, buf, slab_view).run()
    store = pltpu.make_async_copy(buf, theirs, local.at[7])
    store.start()
    links.arrived("small", got_small.at[1], device)
    all_small[1 - place.pipe] = got_small[1]
    keep.wait()
    store.wait()
    links.finish()


def load_layer(l, place, mine, theirs, w, sem):
    pl.when(place.pipe == l)(lambda: pltpu.make_async_copy(mine, w, sem).start())
    pl.when(place.pipe != l)(lambda: pltpu.make_async_copy(theirs, w, sem).start())
    return pltpu.make_async_copy(mine, w, sem)


ORDER_F = ((0, -1), (0, 1), (-1, 0), (1, 0), (-1, -1), (-1, 1), (1, -1), (1, 1), (0, 2), (2, 0), (-1, 2), (2, -1), (1, 2), (2, 1), (2, 2))
ORDER_B = ((2, 2), (0, 2), (2, 0), (-1, 2), (1, 2), (2, -1), (2, 1), (-1, -1), (-1, 1), (1, -1), (1, 1), (0, -1), (0, 1), (-1, 0), (1, 0))


def forward_kernel(
    l, x_ref, slab, slab2, small, tab, y_ref, xg_o, kv_o, q_o, ot_o, lse_o, inner_o,
    w, xg, kvb, acc, top, total, part, rounded, landing, send_sems, recv_sems, local,
):
    place = Place()
    links = Links(send_sems, recv_sems)
    load = load_layer(l, place, slab, slab2, w, local.at[0])
    place.greet(mates=(1, 2, 3))
    mates_gather(place, links, x_ref, xg, "x")
    vectors = small[l].astype(F32)
    mates_gathered(place, links, xg, "x")
    xg_o[...] = xg[...]
    x = jnp.concatenate([xg[0], xg[1]], axis=1).astype(F32)
    normed, _ = normalize(x)
    first = (normed * vectors[0:1] + vectors[2:3]).astype(BF)
    second = (normed * vectors[1:2] + vectors[3:4]).astype(BF)
    load.wait()
    kv = dot(first, w[KV0:Q0, :], NT) + vectors[4:5, 0:384]
    for h in range(3):
        tile = kv[:, h * 128 : h * 128 + 128]
        kvb[place.chip, :, h * 128 : h * 128 + 128] = turn(tile, tab, h != 1, h == 1).astype(BF)
    gather = Gather(place, links, kvb, kv_view)
    gather.begin()
    low, high = lane_mask(True), lane_mask(False)
    qa = dot(first, w[Q0 : Q0 + 128, :], NT) + vectors[4:5, 384:512]
    qb = dot(first, w[Q0 + 64 : Q0 + 192, :], NT)
    qa = (turn(qa, tab, True, True)).astype(BF) * HD**-0.5
    qb = pltpu.roll(qb, 64, 1) + vectors[4:5, 512:640]
    qb = (turn(qb, tab, True, False)).astype(BF) * HD**-0.5
    zero = jnp.zeros((ROWS, 128), BF)
    q_o[0] = jnp.where(low, qa, zero)
    q_o[1] = jnp.where(high, qa, zero)
    q_o[2] = jnp.where(low, qb, zero)
    gather.first()
    inner = dot(second, w[I0:U0, :]) + vectors[5:6]
    inner_o[...] = inner
    act = (inner * (0.5 * (1.0 + lax.erf(inner * (2.0**-0.5))))).astype(BF)
    gather.second()
    branch = dot(act, w[U0:SLAB, :])
    part[0] = branch[:, 0:384]
    part[1] = branch[:, 384:768]

    def scores(kk, h):
        keys = kvb[kk, :, h * 128 : h * 128 + 128]
        return keys, dot(keys, q_o[h], NT)

    causal = lax.broadcasted_iota(jnp.int32, (ROWS, ROWS), 0) <= lax.broadcasted_iota(
        jnp.int32, (ROWS, ROWS), 1
    )
    for h in range(3):
        keys, s = scores(place.chip, h)
        s = jnp.where(causal, s, -1e30)
        m = jnp.max(s, axis=0, keepdims=True)
        p = jnp.exp(s - m)
        top[h] = m
        total[h] = jnp.sum(p, axis=0, keepdims=True)
        acc[h] = dot(keys, p.astype(BF), TN)

    def step(n, carry):
        for j, action in (
            (0, lambda: gather.third(0)),
            (4, lambda: gather.third(-1)),
            (5, lambda: gather.third(1)),
            (8, lambda: gather.fourth(0)),
            (9, lambda: gather.third(2)),
            (10, lambda: gather.fourth(-1)),
            (12, lambda: gather.fourth(1)),
            (14, lambda: gather.fourth(2)),
        ):
            pl.when(n == j)(action)
        kk = place.slot(pick(n, [o[0] for o in ORDER_F]), pick(n, [o[1] for o in ORDER_F]))

        @pl.when(kk < place.chip)
        def _():
            for h in range(3):
                keys, s = scores(kk, h)
                old = top[h]
                m = jnp.maximum(old, jnp.max(s, axis=0, keepdims=True))
                p = jnp.exp(s - m)
                fade = jnp.exp(old - m)
                top[h] = m
                total[h] = total[h] * fade + jnp.sum(p, axis=0, keepdims=True)
                acc[h] = acc[h] * fade + dot(keys, p.astype(BF), TN)

        return carry

    lax.fori_loop(0, 15, step, 0)
    store = pltpu.make_async_copy(kvb, kv_o, local.at[1])
    store.start()
    heads = []
    for h in range(3):
        rows = slice(0, 64) if h == 1 else slice(64, 128)
        heads.append(acc[h, rows, :] / total[h])
        lse_o[h : h + 1, :] = top[h] + jnp.log(total[h])
    attn = jnp.concatenate([heads[1], heads[0], heads[2]], axis=0)
    ot_o[...] = attn
    branch = dot(attn.astype(BF), w[O0:I0, :], TN)
    part[0] = part[0] + branch[:, 0:384]
    part[1] = part[1] + branch[:, 384:768]
    mates_scatter(place, links, part, rounded, landing, "y")
    y = mates_scattered(place, links, part, landing, "y")
    y_ref[...] = (y + x_ref[...].astype(F32) + vectors[6:7, 0:384]).astype(BF)
    store.wait()
    links.finish()


def backward_kernel(
    l, g_ref, xg, slab, slab2, small, tab, tabt, kv, q, ot, lse, inner, gx_ref, wg, sg,
    w, gg, kvb, dkv, dqt, do, first, second, act, slope, part, rounded, landing,
    r1, r2, u1, u2, send_sems, recv_sems, local,
):
    place = Place()
    links = Links(send_sems, recv_sems)
    load = load_layer(l, place, slab, slab2, w, local.at[0])
    load_kv = pltpu.make_async_copy(kv, kvb, local.at[1])
    load_kv.start()
    place.greet(mates=(1, 2, 3))
    mates_gather(place, links, g_ref, gg, "g")
    vectors = small[l].astype(F32)
    x = jnp.concatenate([xg[0], xg[1]], axis=1).astype(F32)
    normed, scale = normalize(x)
    first[...] = (normed * vectors[0:1] + vectors[2:3]).astype(BF)
    second[...] = (normed * vectors[1:2] + vectors[3:4]).astype(BF)
    value = inner[...]
    cdf = 0.5 * (1.0 + lax.erf(value * (2.0**-0.5)))
    act[...] = (value * cdf).astype(BF)
    slope[...] = cdf + value * jnp.exp(-0.5 * value * value) * 0.3989422804014327
    load.wait()
    mates_gathered(place, links, gg, "g")
    g = jnp.concatenate([gg[0], gg[1]], axis=1)
    low, high = lane_mask(True), lane_mask(False)
    zero = jnp.zeros((ROWS, 128), BF)
    da = dot(g, w[O0 : O0 + 128, :], NT).astype(BF)
    db = dot(g, w[O0 + 64 : O0 + 192, :], NT).astype(BF)
    do[0] = jnp.where(high, da, zero)
    do[1] = jnp.where(low, da, zero)
    do[2] = jnp.where(high, db, zero)
    dot_t = dot(w[O0:I0, :], g, NT).astype(BF).astype(F32) * ot[...]
    delta = [
        jnp.sum(dot_t[s : s + 64], axis=0, keepdims=True) for s in (64, 0, 128)
    ]
    load_kv.wait()
    dqt[...] = jnp.zeros_like(dqt)
    scatter = Scatter(place, links, dkv, kv_view, r1, r2, u1, u2)

    def chunk(kk, mask):
        for h in range(3):
            keys = kvb[kk, :, h * 128 : h * 128 + 128]
            p = jnp.exp(dot(keys, q[h], NT) - lse[h : h + 1, :])
            if mask is not None:
                p = jnp.where(mask, p, 0.0)
            dp = dot(keys, do[h], NT)
            ds = (p * (dp - delta[h])).astype(BF)
            dkv[kk, :, h * 128 : h * 128 + 128] = (dot(ds, q[h]) + dot(p.astype(BF), do[h])).astype(BF)
            dqt[h] = dqt[h] + dot(keys, ds, TN)

    def events(j):
        a, b = ORDER_B[j]
        if b == 2:
            for s in (1, -1):
                scatter.v1(0, s, a)
        if a == 2:
            for s in (1, -1):
                scatter.v1(1, s, b)
        if j == 7:
            for s in (1, -1):
                scatter.v2(0, s, 2)
                scatter.v2(1, s, 2)
        if j >= 7:
            if b in (1, -1):
                scatter.v2(0, b, a)
            if a in (1, -1):
                scatter.v2(1, a, b)

    def step(n, carry):
        kk = place.slot(pick(n, [o[0] for o in ORDER_B]), pick(n, [o[1] for o in ORDER_B]))

        @pl.when(kk < place.chip)
        def _():
            chunk(kk, None)

        @pl.when(kk > place.chip)
        def _():
            dkv[kk] = jnp.zeros((ROWS, 384), BF)

        for j in range(15):
            pl.when(n == j)(functools.partial(events, j))
        return carry

    lax.fori_loop(0, 15, step, 0)
    chunk(
        place.chip,
        lax.broadcasted_iota(jnp.int32, (ROWS, ROWS), 0)
        <= lax.broadcasted_iota(jnp.int32, (ROWS, ROWS), 1),
    )
    g = jnp.concatenate([gg[0], gg[1]], axis=1)
    grad_inner = (dot(g, w[U0:SLAB, :], NT) * slope[...]).astype(BF)
    wg[U0:SLAB, :] = dot(act[...], g, TN).astype(BF)
    scatter.tail_one()
    wg[I0:U0, :] = dot(second[...], grad_inner, TN).astype(BF)
    scatter.tail_two()
    grad_second = dot(grad_inner, w[I0:U0, :], NT)
    wg[O0:I0, :] = dot(ot[...].astype(BF), g).astype(BF)
    scatter.tail_three()
    sg[0:1, :] = jnp.sum(grad_second * normed, axis=0, keepdims=True)
    sg[1:2, :] = jnp.sum(grad_second, axis=0, keepdims=True)
    sg[2:3, :] = jnp.sum(grad_inner.astype(F32), axis=0, keepdims=True)
    sg[3:4, :] = jnp.sum(g.astype(F32), axis=0, keepdims=True)
    sg[6:8, :] = jnp.zeros((2, D), F32)
    rows = []
    for h in range(3):
        base = 64 if h == 1 else 0
        dq = dqt[h, base : base + 64, :] * HD**-0.5
        a, b = dq[0:8], dq[8:16]
        rows += [a * tabt[0] + b * tabt[1], b * tabt[0] - a * tabt[1], dq[16:64]]
    dq = jnp.concatenate(rows, axis=0).astype(BF)
    wg[Q0:O0, :] = dot(dq, first[...]).astype(BF)
    grad_first = dot(dq, w[Q0:O0, :], TN)
    q_sums = dot(jnp.ones((8, ROWS), BF), dq, NT)
    pre = jnp.concatenate([scatter.last(0), scatter.last(1)], axis=0)
    tiles = [
        turn(pre[:, h * 128 : h * 128 + 128], tab, h != 1, h == 1, -1.0).astype(BF)
        for h in range(3)
    ]
    pre = jnp.concatenate(tiles, axis=1)
    wg[KV0:Q0, :] = dot(pre, first[...], TN).astype(BF)
    grad_first = grad_first + dot(pre, w[KV0:Q0, :])
    sg[4:5, :] = jnp.sum(grad_first * normed, axis=0, keepdims=True)
    sg[5:6, :] = jnp.sum(grad_first, axis=0, keepdims=True)
    sg[6:7, 0:384] = jnp.sum(pre.astype(F32), axis=0, keepdims=True)
    sg[7:8, 0:192] = q_sums[0:1, :]
    grad_norm = grad_first * vectors[0:1] + grad_second * vectors[1:2]
    grad_x = scale * (
        grad_norm
        - jnp.mean(grad_norm, axis=-1, keepdims=True)
        - normed * jnp.mean(grad_norm * normed, axis=-1, keepdims=True)
    )
    part[0] = grad_x[:, 0:384]
    part[1] = grad_x[:, 384:768]
    mates_scatter(place, links, part, rounded, landing, "gx")
    grad = mates_scattered(place, links, part, landing, "gx")
    gx_ref[...] = (grad + g_ref[...].astype(F32)).astype(BF)
    links.finish()


def grads_kernel(
    wg0, wg1, sg0, sg1, out, out_small, buf, own, other, piece, got, r1, r2, u1, u2,
    sm, along_x, along_z, across, beside, send_sems, recv_sems, local
):
    place = Place()
    links = Links(send_sems, recv_sems)
    load_theirs = load_layer(1, place, wg0, wg1, other, local.at[0])
    load_mine = load_layer(0, place, wg0, wg1, own, local.at[1])
    place.greet(mates=(1, 2, 3), partner=True, far=True)
    sm[0, 0] = sg0[...]
    sm[0, 1] = sg1[...]
    for d in (1, 2, 3):
        links.send(("sx", d), lambda d=d: (sm.at[0], along_x.at[d - 1], place.at(d, 0)))

    def small_z():
        total = sm[0]
        for d in (1, 2, 3):
            links.arrived(("sx", d), along_x.at[d - 1], place.at(d, 0))
            total = total + along_x[d - 1]
        sm[1] = total
        for d in (1, 2, 3):
            links.send(("sz", d), lambda d=d: (sm.at[1], along_z.at[d - 1], place.at(0, d)))

    def small_pipe():
        total = sm[1]
        for d in (1, 2, 3):
            links.arrived(("sz", d), along_z.at[d - 1], place.at(0, d))
            total = total + along_z[d - 1]
        sm[2] = total
        links.send("sp", lambda: (sm.at[2, 1 - place.pipe], across, place.partner()))

    def small_mates():
        links.arrived("sp", across, place.partner())
        sm[3, 0] = sm[2, place.pipe] + across[...]
        for r in (1, 2, 3):
            links.send(("sm", r), lambda r=r: (sm.at[3, 0], beside.at[r - 1], place.mate(r)[2]))

    def small_last():
        total = sm[3, 0]
        for r in (1, 2, 3):
            links.arrived(("sm", r), beside.at[r - 1], place.mate(r)[2])
            total = total + beside[r - 1]
        row = lax.broadcasted_iota(jnp.int32, (8, D), 0)
        norm = (row < 2) | ((row >= 4) & (row < 6))
        out_small[place.core] = jnp.where(norm, total, sm[3, 0])
        out_small[1 - place.core] = jnp.where(norm, total, beside[0])

    sums = []
    for i, ref in ((0, other), (1, own)):
        (load_theirs, load_mine)[i].wait()
        scatter = Scatter(place, links, ref, slab_view, r1.at[i], r2.at[i], u1.at[i], u2.at[i], i)
        sums.append(scatter)
        for du in (2, -1, 1, 0):
            for h in (0, 1):
                for s in (1, -1):
                    scatter.v1(h, s, du)
    small_z()
    for scatter in sums:
        for du in (2, -1, 1, 0):
            for h in (0, 1):
                for s in (1, -1):
                    scatter.v2(h, s, du)
    small_pipe()
    device = place.partner()
    for i, scatter in enumerate(sums):
        scatter.tail_one()
        scatter.tail_two()
        scatter.tail_three()
        for h in (0, 1):
            piece[i, :, h * 384 : h * 384 + 384] = scatter.last(h)
        if i == 0:
            got[0] = piece[0].astype(BF)
            links.send("piece", lambda: (got.at[0], got.at[1], device))
    links.arrived("piece", got.at[1], device)
    small_mates()
    buf[place.core, place.chip] = (piece[1] + got[1].astype(F32)).astype(BF)
    sibling = place.mate(1)[2]

    def pass_on(a, b):
        ref = lambda: buf.at[place.core, place.slot(a, b)]
        links.send(("core", a, b), lambda: (ref(), ref(), sibling))

    Gather(place, links, buf.at[place.core], slab_view, "g").run(pass_on)
    keep = pltpu.make_async_copy(buf.at[place.core], out.at[place.core], local.at[0])
    keep.start()
    small_last()
    for a, b in ((0, 0), *ORDER_F):
        links.arrived(("core", a, b), buf.at[1 - place.core, place.slot(a, b)], sibling)
    rest = pltpu.make_async_copy(buf.at[1 - place.core], out.at[1 - place.core], local.at[1])
    rest.start()
    keep.wait()
    rest.wait()
    links.finish()


VMEM = pl.BlockSpec(memory_space=pltpu.VMEM)
ANY = pl.BlockSpec(memory_space=pl.ANY)


def sems(n, m):
    return [pltpu.SemaphoreType.DMA((n,)), pltpu.SemaphoreType.DMA((n,)), pltpu.SemaphoreType.DMA((m,))]


def shape(dims, kind=BF):
    return jax.ShapeDtypeStruct(dims, kind)


def params(i):
    return pltpu.CompilerParams(collective_id=i, has_side_effects=True, vmem_limit_bytes=56 * 2**20)


def share_weights(*args):
    return pl.pallas_call(
        weights_kernel,
        name="share_weights",
        out_shape=(shape((SLAB, D)), shape((CHIPS, PIECE, D)), shape((2, 16, D))),
        in_specs=[ANY, ANY, ANY, ANY, VMEM, VMEM, VMEM, VMEM, VMEM],
        out_specs=(ANY, ANY, VMEM),
        scratch_shapes=[
            pltpu.VMEM((SLAB, D), BF),
            pltpu.VMEM((CHIPS, PIECE, D), BF),
            pltpu.VMEM((3, D, 384), BF),
            pltpu.VMEM((384, D), BF),
            pltpu.VMEM((16, D), F32),
            pltpu.VMEM((2, 16, D), BF),
            *sems(48, 8),
        ],
        compiler_params=params(0),
    )(*args)


def forward(l, x, slab, small, tab):
    return pl.pallas_call(
        functools.partial(forward_kernel, l),
        name=f"layer_{l}_forward",
        out_shape=(
            shape((128, 384)),
            shape((2, ROWS, 384)),
            shape((CHIPS, ROWS, 384)),
            shape((3, ROWS, 128)),
            shape((192, ROWS), F32),
            shape((8, ROWS), F32),
            shape((ROWS, D), F32),
        ),
        in_specs=[VMEM, ANY, ANY, VMEM, VMEM],
        out_specs=(VMEM, VMEM, ANY, VMEM, VMEM, VMEM, VMEM),
        scratch_shapes=[
            pltpu.VMEM((SLAB, D), BF),
            pltpu.VMEM((2, ROWS, 384), BF),
            pltpu.VMEM((CHIPS, ROWS, 384), BF),
            pltpu.VMEM((3, 128, ROWS), F32),
            pltpu.VMEM((3, 1, ROWS), F32),
            pltpu.VMEM((3, 1, ROWS), F32),
            pltpu.VMEM((2, ROWS, 384), F32),
            pltpu.VMEM((2, ROWS, 384), BF),
            pltpu.VMEM((3, 128, 384), BF),
            *sems(48, 2),
        ],
        compiler_params=params(1 + l),
    )(x, *slab, small, tab)


def landing_shapes(rows, part, lead=()):
    return [
        pltpu.VMEM((*lead, 2, 2, 4, part, 384), BF),
        pltpu.VMEM((*lead, 2, 2, 4, rows, 384), BF),
        pltpu.VMEM((*lead, 2, 2, part, 384), BF),
        pltpu.VMEM((*lead, 2, 2, rows, 384), BF),
    ]


def backward(l, g, kept, slab, small, tab, tabt):
    xg, kv, q, ot, lse, inner = kept
    return pl.pallas_call(
        functools.partial(backward_kernel, l),
        name=f"layer_{l}_backward",
        out_shape=(shape((128, 384)), shape((SLAB, D)), shape((8, D), F32)),
        in_specs=[VMEM, VMEM, ANY, ANY, VMEM, VMEM, VMEM, ANY, VMEM, VMEM, VMEM, VMEM],
        out_specs=(VMEM, VMEM, VMEM),
        scratch_shapes=[
            pltpu.VMEM((SLAB, D), BF),
            pltpu.VMEM((2, ROWS, 384), BF),
            pltpu.VMEM((CHIPS, ROWS, 384), BF),
            pltpu.VMEM((CHIPS, ROWS, 384), BF),
            pltpu.VMEM((3, 128, ROWS), F32),
            pltpu.VMEM((3, ROWS, 128), BF),
            pltpu.VMEM((ROWS, D), BF),
            pltpu.VMEM((ROWS, D), BF),
            pltpu.VMEM((ROWS, D), BF),
            pltpu.VMEM((ROWS, D), F32),
            pltpu.VMEM((2, ROWS, 384), F32),
            pltpu.VMEM((2, ROWS, 384), BF),
            pltpu.VMEM((3, 128, 384), BF),
            *landing_shapes(128, 64),
            *sems(56, 2),
        ],
        compiler_params=params(3 + l),
    )(g, xg, *slab, small, tab, tabt, kv, q, ot, lse, inner)


def share_grads(*args):
    return pl.pallas_call(
        grads_kernel,
        name="share_grads",
        out_shape=(shape((2, CHIPS, PIECE, D)), shape((2, 8, D), F32)),
        in_specs=[ANY, ANY, VMEM, VMEM],
        out_specs=(ANY, VMEM),
        scratch_shapes=[
            pltpu.VMEM((2, CHIPS, PIECE, D), BF),
            pltpu.VMEM((CHIPS, PIECE, D), BF),
            pltpu.VMEM((CHIPS, PIECE, D), BF),
            pltpu.VMEM((2, PIECE, D), F32),
            pltpu.VMEM((2, PIECE, D), BF),
            *landing_shapes(PIECE, 80, (2,)),
            pltpu.VMEM((4, 2, 8, D), F32),
            pltpu.VMEM((3, 2, 8, D), F32),
            pltpu.VMEM((3, 2, 8, D), F32),
            pltpu.VMEM((8, D), F32),
            pltpu.VMEM((3, 8, D), F32),
            *sems(160, 2),
        ],
        compiler_params=params(5),
    )(*args)


def finish_kernel(
    whole, small, g_qkv, g_out, g_in, g_down, g_gain, g_shift, g_qkv_b, g_out_b, g_in_b,
    held, qkv, out, wide, down, local,
):
    regions = ((U0, SLAB), (I0, U0), (O0, I0), (KV0, O0))
    loads = []
    for i, (lo, hi) in enumerate(regions):
        for c in (0, 1):
            rows = pl.ds(lo, hi - lo)
            load = pltpu.make_async_copy(whole.at[c, rows], held.at[c, rows], local.at[2 * i + c])
            load.start()
            loads.append(load)
    tensor = lax.axis_index("tensor")
    rows = [small[0], small[1]]

    def features(row):
        return jnp.where(tensor == 0, row[:, 0:384], row[:, 384:768])

    g_gain[0:1] = features(rows[0][4:5])
    g_gain[1:2] = features(rows[0][0:1])
    g_shift[0:1] = features(rows[0][5:6])
    g_shift[1:2] = features(rows[0][1:2])
    g_out_b[...] = features(rows[0][3:4])
    g_in_b[...] = jnp.concatenate([rows[0][2:3], rows[1][2:3]], axis=1)
    for j in range(3):
        pieces = []
        for c in (0, 1):
            for i in [BLOCKS.index((j, h)) for h in range(3)]:
                row, at = (6, i) if i < 6 else (7, i - 6)
                pieces.append(rows[c][row : row + 1, at * 64 : at * 64 + 64])
        g_qkv_b[j : j + 1] = jnp.concatenate(pieces, axis=1)
    stores = []

    def store(i, src, dst):
        copy = pltpu.make_async_copy(src, dst, local.at[8 + i])
        copy.start()
        stores.append(copy)

    for c in (0, 1):
        loads[c].wait()
        down[c * 768 : c * 768 + 768] = held[c, U0:SLAB].astype(F32)
        store(c, down.at[pl.ds(c * 768, 768)], g_down.at[pl.ds(c * 768, 768)])
    for c in (0, 1):
        loads[2 + c].wait()
        wide[:, c * 768 : c * 768 + 768] = held[c, I0:U0].astype(F32)
    store(2, wide, g_in)
    for c in (0, 1):
        loads[4 + c].wait()
        for i, block in enumerate((1, 0, 2)):
            start = c * 192 + block * 64
            out[start : start + 64] = held[c, O0 + i * 64 : O0 + i * 64 + 64].astype(F32)
    store(3, out, g_out)
    for c in (0, 1):
        loads[6 + c].wait()
    for j in range(3):
        pieces = []
        for c in (0, 1):
            for i in [BLOCKS.index((j, h)) for h in range(3)]:
                pieces.append(held[c, i * 64 : i * 64 + 64])
        qkv[j] = jnp.concatenate(pieces, axis=0).astype(F32).T
        store(4 + j, qkv.at[j], g_qkv.at[j])
    for copy in stores:
        copy.wait()


def finish(whole, small):
    return pl.pallas_call(
        finish_kernel,
        name="finish",
        out_shape=(
            shape((3, D, 384), F32),
            shape((384, D), F32),
            shape((D, 1536), F32),
            shape((1536, D), F32),
            shape((2, 384), F32),
            shape((2, 384), F32),
            shape((3, 384), F32),
            shape((1, 384), F32),
            shape((1, 1536), F32),
        ),
        in_specs=[ANY, VMEM],
        out_specs=(ANY, ANY, ANY, ANY, VMEM, VMEM, VMEM, VMEM, VMEM),
        scratch_shapes=[
            pltpu.VMEM((2, SLAB, D), BF),
            pltpu.VMEM((3, D, 384), F32),
            pltpu.VMEM((384, D), F32),
            pltpu.VMEM((D, 1536), F32),
            pltpu.VMEM((1536, D), F32),
            pltpu.SemaphoreType.DMA((16,)),
        ],
        compiler_params=pltpu.CompilerParams(vmem_limit_bytes=56 * 2**20),
    )(whole, small)


def rope_tables(chip):
    half = HD // 8
    freqs = 10000.0 ** (-2.0 * jnp.arange(half, dtype=F32) / (2 * half))
    positions = chip * ROWS + jnp.arange(ROWS, dtype=jnp.int32)
    angles = positions.astype(F32)[:, None] * freqs[None, :]
    cosine, sine = jnp.cos(angles), jnp.sin(angles)
    none = jnp.zeros((ROWS, half), F32)
    rest = jnp.zeros((ROWS, HD - 2 * half), F32)
    tiles = [
        jnp.concatenate([cosine, cosine, rest + 1.0], axis=1),
        jnp.concatenate([none, sine, rest], axis=1),
        jnp.concatenate([-sine, none, rest], axis=1),
    ]
    tab = jnp.stack([jnp.concatenate([tile, tile], axis=1) for tile in tiles])
    return tab, jnp.stack([cosine.T, sine.T])


def body(
    inputs, cotangent, ln_gain, ln_bias, qkv_weight, qkv_bias, out_weight, out_bias,
    fc_in_weight, fc_in_bias, fc_out_weight,
):
    pipe = lax.axis_index("pipe")
    ctx = lax.axis_index("ctx")
    tab, tabt = rope_tables(ctx // 2)
    mine, theirs, smalls = share_weights(
        qkv_weight[0], out_weight[0], fc_in_weight[0], fc_out_weight[0], ln_gain[0], ln_bias[0],
        qkv_bias[0], fc_in_bias, out_bias,
    )
    slabs = mine, theirs.reshape(SLAB, D)

    x = lax.dynamic_index_in_dim(inputs, pipe, 0, keepdims=False)
    g = lax.dynamic_index_in_dim(cotangent, pipe, 0, keepdims=False)
    middle, *kept0 = forward(0, x, slabs, smalls, tab)
    upper, *kept1 = forward(1, middle, slabs, smalls, tab)
    g, wg1, sg1 = backward(1, g, kept1, slabs, smalls, tab, tabt)
    g, wg0, sg0 = backward(0, g, kept0, slabs, smalls, tab, tabt)

    lower_pipe = pipe == 0
    sent = jnp.where(lower_pipe, upper, g)
    held = jnp.where(lower_pipe, g, upper)
    got = lax.ppermute(sent, "pipe", [(0, 1), (1, 0)])
    boundary = jnp.stack([jnp.where(lower_pipe, held, got), jnp.where(lower_pipe, got, held)])[None]

    whole, sums = share_grads(
        wg0.reshape(CHIPS, PIECE, D), wg1.reshape(CHIPS, PIECE, D), sg0, sg1
    )
    g_qkv, g_out, g_in, g_down, g_gain, g_shift, g_qkv_b, g_out_b, g_in_b = finish(
        whole.reshape(2, SLAB, D), sums
    )
    return (
        boundary,
        g_gain[None],
        g_shift[None],
        g_qkv[None],
        g_qkv_b[None],
        g_out[None],
        g_out_b,
        g_in[None],
        g_in_b,
        g_down[None],
    )


def solution(mesh):
    return jax.shard_map(
        body,
        mesh=mesh,
        in_specs=(
            P(None, "ctx", "tensor"),
            P(None, "ctx", "tensor"),
            P("pipe", None, None),
            P("pipe", None, None),
            P("pipe", None, None, "tensor"),
            P("pipe", None, "tensor"),
            P("pipe", "tensor", None),
            P("pipe", "tensor"),
            P("pipe", None, "tensor"),
            P("pipe", "tensor"),
            P("pipe", "tensor", None),
        ),
        out_specs=(
            P("pipe", None, "ctx", "tensor"),
            P("pipe", None, "tensor"),
            P("pipe", None, "tensor"),
            P("pipe", None, None, "tensor"),
            P("pipe", None, "tensor"),
            P("pipe", "tensor", None),
            P("pipe", "tensor"),
            P("pipe", None, "tensor"),
            P("pipe", "tensor"),
            P("pipe", "tensor", None),
        ),
        check_vma=False,
    )
```

```python
import functools

import jax
import jax.numpy as jnp
from jax import lax
from jax.experimental import pallas as pl
from jax.experimental.pallas import tpu as pltpu
from jax.sharding import PartitionSpec as P


D = 768
HD = 64
F32 = jnp.float32
BF = jnp.bfloat16
MESH = pl.DeviceIdType.MESH
EPS = 1e-05
CHIPS = 16
ROWS = 256
PIECE = 144
SLAB = CHIPS * PIECE
KV0, Q0, O0, I0, U0 = 0, 384, 576, 768, 1536
BLOCKS = ((1, 0), (2, 0), (2, 1), (1, 1), (1, 2), (2, 2), (0, 0), (0, 1), (0, 2))
NN = (((1,), (0,)), ((), ()))
NT = (((1,), (1,)), ((), ()))
TN = (((0,), (0,)), ((), ()))


def dot(a, b, dims=NN):
    return lax.dot_general(a, b, dims, preferred_element_type=F32)


class Place:
    def __init__(self):
        self.pipe = lax.axis_index("pipe")
        self.tensor = lax.axis_index("tensor")
        ctx = lax.axis_index("ctx")
        self.core = lax.rem(ctx, 2)
        self.chip = ctx // 2
        self.x = self.chip // 4
        self.z = lax.rem(self.chip, 4)

    def slot(self, dx, dz):
        return lax.rem(self.x + (dx + 4), 4) * 4 + lax.rem(self.z + (dz + 4), 4)

    def at(self, dx, dz):
        return (self.pipe, self.tensor, self.slot(dx, dz) * 2 + self.core)

    def mate(self, r):
        t = lax.rem(self.tensor + r // 2, 2)
        c = lax.rem(self.core + r % 2, 2)
        return t, c, (self.pipe, t, self.chip * 2 + c)

    def partner(self):
        return (1 - self.pipe, self.tensor, self.chip * 2 + self.core)

    def greet(self, mates=(), partner=False, far=False):
        bar = pltpu.get_barrier_semaphore()
        targets = [self.at(1, 0), self.at(-1, 0), self.at(0, 1), self.at(0, -1)]
        if far:
            targets += [self.at(2, 0), self.at(0, 2)]
        targets += [self.mate(r)[2] for r in mates]
        if partner:
            targets.append(self.partner())
        for target in targets:
            pl.semaphore_signal(bar, inc=1, device_id=target, device_id_type=MESH)
        pl.semaphore_wait(bar, len(targets))


class Links:
    def __init__(self, send_sems, recv_sems):
        self.send_sems, self.recv_sems = send_sems, recv_sems
        self.ids, self.sent = {}, []

    def desc(self, key, src, dst, device):
        i = self.ids.setdefault(key, len(self.ids))
        return pltpu.make_async_remote_copy(
            src_ref=src,
            dst_ref=dst,
            send_sem=self.send_sems.at[i],
            recv_sem=self.recv_sems.at[i],
            device_id=device,
            device_id_type=MESH,
        )

    def send(self, key, copy):
        self.desc(key, *copy()).start()
        self.sent.append((key, copy))

    def arrived(self, key, dst, device):
        self.desc(key, dst, dst, device).wait_recv()

    def finish(self):
        for key, copy in self.sent:
            self.desc(key, *copy()).wait_send()


def kv_view(h, part):
    start, size = {"all": (0, 128), 0: (0, 64), 1: (64, 64)}[part]
    return (pl.ds(h * 128 + start, size), pl.ds(0, 384))


def slab_view(h, part, base=0, rows=PIECE):
    cut = (rows // 2 + 8) // 16 * 16
    cut = rows - cut if h else cut
    start, size = {"all": (0, rows), 0: (0, cut), 1: (cut, rows - cut)}[part]
    return (pl.ds(base + start, size), pl.ds(h * 384, 384))


PARTS = ((0, 80), (80, 64))


def part_view(i):
    return lambda h, part: slab_view(h, part, *PARTS[i])


class Gather:
    def __init__(self, place, links, buf, view, tag=""):
        self.place, self.links, self.buf, self.view, self.tag = place, links, buf, view, tag

    def ref(self, du, dv, h, part):
        slot = self.place.slot(du, dv) if h == 0 else self.place.slot(dv, du)
        return self.buf.at[(slot,) + self.view(h, part)]

    def dev(self, along_u, step, h):
        return self.place.at(step, 0) if along_u == (h == 0) else self.place.at(0, step)

    def snd(self, h, along_u, step, du, dv, part):
        key = (self.tag, h, along_u, step, du - (step if along_u else 0), dv - (0 if along_u else step), part)
        ref = lambda: self.ref(du, dv, h, part)
        self.links.send(key, lambda: (ref(), ref(), self.dev(along_u, step, h)))

    def rcv(self, h, along_u, step, du, dv, part):
        key = (self.tag, h, along_u, step, du, dv, part)
        self.links.arrived(key, self.ref(du, dv, h, part), self.dev(along_u, step, h))

    def begin(self):
        for h in (0, 1):
            for step in (1, -1):
                self.snd(h, True, step, 0, 0, "all")

    def own_line(self):
        for h in (0, 1):
            for step in (1, -1):
                self.snd(h, False, step, 0, 0, "all")

    def first(self):
        for h in (0, 1):
            for step, part in ((1, 0), (-1, 1)):
                self.rcv(h, True, step, -step, 0, "all")
                self.snd(h, True, step, -step, 0, part)
                for s in (1, -1):
                    self.snd(h, False, s, -step, 0, "all")

    def second(self):
        for h in (0, 1):
            for step, part in ((1, 0), (-1, 1)):
                self.rcv(h, True, step, -2 * step, 0, part)
            for s in (1, -1):
                self.snd(h, False, s, 2, 0, "all")

    def third(self, du):
        for h in (0, 1):
            for step, part in ((1, 0), (-1, 1)):
                self.rcv(h, False, step, du, -step, "all")
                self.snd(h, False, step, du, -step, part)

    def fourth(self, du):
        for h in (0, 1):
            for step, part in ((1, 0), (-1, 1)):
                self.rcv(h, False, step, du, -2 * step, part)


def gather_parts(parts, arrived, done=lambda a, b: None):
    for i, part in enumerate(parts):
        arrived(i)
        part.begin()
    done(0, 0)
    for part in parts:
        part.first()
        part.own_line()
    for part in parts:
        part.second()
    for stage, du, slots in (
        ("third", 0, ORDER_F[0:4]),
        ("third", -1, ORDER_F[4:5]),
        ("third", 1, ORDER_F[5:8]),
        ("third", 2, ()),
        ("fourth", 0, ORDER_F[8:10]),
        ("fourth", -1, ORDER_F[10:12]),
        ("fourth", 1, ORDER_F[12:14]),
        ("fourth", 2, ORDER_F[14:15]),
    ):
        for part in parts:
            getattr(part, stage)(du)
        for a, b in slots:
            done(a, b)


class Scatter:
    def __init__(self, place, links, buf, view, r1, r2, u1, u2, tag=""):
        self.place, self.links, self.buf, self.view = place, links, buf, view
        self.r1, self.r2, self.u1, self.u2, self.tag = r1, r2, u1, u2, tag

    def ref(self, du, dv, h, part):
        slot = self.place.slot(du, dv) if h == 0 else self.place.slot(dv, du)
        return self.buf.at[(slot,) + self.view(h, part)]

    def dev(self, along_u, step, h):
        return self.place.at(step, 0) if along_u == (h == 0) else self.place.at(0, step)

    def size(self, h, part):
        return pl.ds(0, self.view(h, part)[0].size)

    def land(self, stage, h, step, du):
        d, e = (step + 1) // 2, (du + 4) % 4
        part = (1 - d) if stage in ("v1", "u1") else "all"
        rows = self.size(h, part)
        return {
            "v1": lambda: self.r1.at[h, d, e, rows],
            "v2": lambda: self.r2.at[h, d, e, rows],
            "u1": lambda: self.u1.at[h, d, rows],
            "u2": lambda: self.u2.at[h, d, rows],
        }[stage]()

    def snd(self, stage, h, step, du, src):
        key = (self.tag, stage, h, step, du)
        device = lambda: self.dev(stage[0] == "u", step, h)
        self.links.send(key, lambda: (src(), self.land(stage, h, step, du), device()))

    def rcv(self, stage, h, step, du):
        ref = self.land(stage, h, step, du)
        self.links.arrived((self.tag, stage, h, step, du), ref, self.dev(stage[0] == "u", step, h))
        return ref

    def v1(self, h, step, du):
        self.snd("v1", h, step, du, lambda: self.ref(du, 2, h, (1 - step) // 2))

    def v2(self, h, step, du):
        got = self.rcv("v1", h, step, du)
        mine = self.ref(du, step, h, (1 - step) // 2)
        mine[...] = (mine[...].astype(F32) + got[...].astype(F32)).astype(BF)
        self.snd("v2", h, step, du, lambda: self.ref(du, step, h, "all"))

    def vsum(self, h, du):
        one, two = self.rcv("v2", h, 1, du), self.rcv("v2", h, -1, du)
        mine = self.ref(du, 0, h, "all")
        mine[...] = (mine[...].astype(F32) + one[...].astype(F32) + two[...].astype(F32)).astype(BF)

    def u1s(self, h):
        for step in (1, -1):
            self.snd("u1", h, step, 0, lambda step=step: self.ref(2, 0, h, (1 - step) // 2))

    def u2s(self, h, step):
        got = self.rcv("u1", h, step, 0)
        mine = self.ref(step, 0, h, (1 - step) // 2)
        mine[...] = (mine[...].astype(F32) + got[...].astype(F32)).astype(BF)
        self.snd("u2", h, step, 0, lambda: self.ref(step, 0, h, "all"))

    def last(self, h):
        one, two = self.rcv("u2", h, 1, 0), self.rcv("u2", h, -1, 0)
        mine = self.ref(0, 0, h, "all")
        return mine[...].astype(F32) + one[...].astype(F32) + two[...].astype(F32)

    def begin(self):
        for du in (2, -1, 1, 0):
            for h in (0, 1):
                for step in (1, -1):
                    self.v1(h, step, du)

    def middle(self):
        for du in (2, -1, 1, 0):
            for h in (0, 1):
                for step in (1, -1):
                    self.v2(h, step, du)

    def tail_one(self):
        for h in (0, 1):
            self.vsum(h, 2)
            self.u1s(h)

    def tail_two(self):
        for h in (0, 1):
            for step in (1, -1):
                self.vsum(h, step)
                self.u2s(h, step)

    def tail_three(self):
        for h in (0, 1):
            self.vsum(h, 0)


def pick(n, values):
    out = 0
    for j, v in enumerate(values):
        out = out + (n == j).astype(jnp.int32) * v
    return out


def mates_gather(place, links, own, full, tag):
    rows = pl.ds(pl.multiple_of(place.core * 128, 128), 128)
    for r in (2, 1):
        device = place.mate(r)[2]
        links.send((tag, r), lambda device=device: (own, full.at[place.tensor, rows], device))
    full[place.tensor, rows] = own[...]


def mates_gathered(place, links, full, tag):
    rows = pl.ds(pl.multiple_of(place.core * 128, 128), 128)
    others = pl.ds(pl.multiple_of(128 - place.core * 128, 128), 128)
    far, sibling = place.mate(2)[2], place.mate(1)[2]
    links.arrived((tag, 2), full.at[1 - place.tensor, rows], far)
    passed = full.at[1 - place.tensor, rows]
    links.send((tag, 3), lambda: (passed, passed, sibling))
    links.arrived((tag, 1), full.at[place.tensor, others], sibling)
    links.arrived((tag, 3), full.at[1 - place.tensor, others], sibling)


def mates_scatter(place, links, part, rounded, landing, tag):
    others = pl.ds(pl.multiple_of(128 - place.core * 128, 128), 128)
    rounded[:, others] = part[:, others].astype(BF)
    device = place.mate(1)[2]
    links.send((tag, 1), lambda: (rounded.at[:, others], landing.at[pl.ds(0, 2)], device))


def mates_scattered(place, links, part, rounded, landing, tag):
    rows = pl.ds(pl.multiple_of(place.core * 128, 128), 128)
    links.arrived((tag, 1), landing.at[pl.ds(0, 2)], place.mate(1)[2])
    away = part[1 - place.tensor, rows] + landing[1 - place.tensor].astype(F32)
    rounded[1 - place.tensor, rows] = away.astype(BF)
    device = place.mate(2)[2]
    links.send((tag, 2), lambda: (rounded.at[1 - place.tensor, rows], landing.at[2], device))
    total = part[place.tensor, rows] + landing[place.tensor].astype(F32)
    links.arrived((tag, 2), landing.at[2], device)
    return total + landing[2].astype(F32)


def normalize(values):
    centered = values - jnp.mean(values, axis=-1, keepdims=True)
    variance = jnp.mean(centered * centered, axis=-1, keepdims=True)
    scale = lax.rsqrt(variance + EPS)
    return centered * scale, scale


def lane_mask(lower, shape=(ROWS, 128)):
    lane = lax.broadcasted_iota(jnp.int32, shape, 1)
    return lane < 64 if lower else lane >= 64


def turn(values, tab, lower, upper, sign=1.0):
    cosine, plus, minus = tab[0], tab[1], tab[2]
    turned = (
        values * cosine
        + sign * (pltpu.roll(values, 8, 1) * plus + pltpu.roll(values, 120, 1) * minus)
    )
    if lower and upper:
        return turned
    return jnp.where(lane_mask(lower), turned, values)


def weights_kernel(
    qkv, out, fc_in, fc_out, gain, shift, qkv_b, in_b, out_b, mine, theirs, all_small,
    own, buf, raw, turned, small, got_small, send_sems, recv_sems, local,
):
    place = Place()
    links = Links(send_sems, recv_sems)
    core = place.core
    loads = [pltpu.make_async_copy(qkv, raw, local.at[0])]
    for i, block in enumerate((1, 0, 2)):
        rows = pl.ds(pl.multiple_of(core * 192 + block * 64, 64), 64)
        loads.append(pltpu.make_async_copy(out.at[rows], own.at[pl.ds(O0 + i * 64, 64)], local.at[1 + i]))
    half = pl.ds(pl.multiple_of(core * 768, 768), 768)
    loads.append(pltpu.make_async_copy(fc_in.at[:, half], own.at[pl.ds(I0, 768)], local.at[4]))
    loads.append(pltpu.make_async_copy(fc_out.at[half], own.at[pl.ds(U0, 768)], local.at[5]))
    for load in loads:
        load.start()
    place.greet(partner=True)
    small[...] = jnp.zeros_like(small)
    small[0:2] = gain[...].astype(F32)
    small[2:4] = shift[...].astype(F32)
    bias = qkv_b[...].astype(F32)
    bias = jnp.where(core == 0, bias[:, 0:192], bias[:, 192:384])
    pieces = [bias[j : j + 1, h * 64 : h * 64 + 64] for j, h in BLOCKS]
    small[4:5, 0:576] = jnp.concatenate(pieces, axis=1)
    wide = in_b[...].astype(F32)
    small[5:6] = jnp.where(core == 0, wide[:, 0:768], wide[:, 768:1536])
    small[6:7, 0:384] = out_b[...].astype(F32)
    rounded = small[...].astype(BF)
    all_small[place.pipe] = rounded
    loads[0].wait()
    for j in range(3):
        turned[...] = raw[j].T
        for i, (k, h) in enumerate(BLOCKS):
            if k == j:
                own[i * 64 : i * 64 + 64, :] = turned[pl.ds(pl.multiple_of(core * 192 + h * 64, 64), 64), :]
    for load in loads[1:]:
        load.wait()
    device = place.partner()
    for i, (base, rows) in enumerate(PARTS):
        src = own.at[pl.ds(pl.multiple_of(place.chip * PIECE + base, 16), rows)]
        dst = buf.at[place.chip, pl.ds(base, rows)]
        links.send(("slab", i), lambda src=src, dst=dst: (src, dst, device))
    got_small[0] = rounded
    links.send("small", lambda: (got_small.at[0], got_small.at[1], device))
    keep = pltpu.make_async_copy(own, mine, local.at[6])
    keep.start()

    def piece(i):
        links.arrived(("slab", i), buf.at[place.chip, pl.ds(*PARTS[i])], device)

    gather_parts([Gather(place, links, buf, part_view(i), i) for i in range(2)], piece)
    store = pltpu.make_async_copy(buf, theirs, local.at[7])
    store.start()
    links.arrived("small", got_small.at[1], device)
    all_small[1 - place.pipe] = got_small[1]
    keep.wait()
    store.wait()
    links.finish()


def load_layer(l, place, mine, theirs, w, sem):
    pl.when(place.pipe == l)(lambda: pltpu.make_async_copy(mine, w, sem).start())
    pl.when(place.pipe != l)(lambda: pltpu.make_async_copy(theirs, w, sem).start())
    return pltpu.make_async_copy(mine, w, sem)


ORDER_F = ((0, -1), (0, 1), (-1, 0), (1, 0), (-1, -1), (-1, 1), (1, -1), (1, 1), (0, 2), (2, 0), (-1, 2), (2, -1), (1, 2), (2, 1), (2, 2))
ORDER_B = ((2, 2), (0, 2), (2, 0), (-1, 2), (1, 2), (2, -1), (2, 1), (-1, -1), (-1, 1), (1, -1), (1, 1), (0, -1), (0, 1), (-1, 0), (1, 0))


def forward_kernel(
    l, x_ref, slab, slab2, small, tab, y_ref, xg_o, kv_o, q_o, ot_o, lse_o, inner_o,
    w, xg, kvb, acc, top, total, part, rounded, landing, send_sems, recv_sems, local,
):
    place = Place()
    links = Links(send_sems, recv_sems)
    load = load_layer(l, place, slab, slab2, w, local.at[0])
    place.greet(mates=(1, 2))
    mates_gather(place, links, x_ref, xg, "x")
    vectors = small[l].astype(F32)
    mates_gathered(place, links, xg, "x")
    xg_o[...] = xg[...]
    x = jnp.concatenate([xg[0], xg[1]], axis=1).astype(F32)
    normed, _ = normalize(x)
    first = (normed * vectors[0:1] + vectors[2:3]).astype(BF)
    second = (normed * vectors[1:2] + vectors[3:4]).astype(BF)
    load.wait()
    kv = dot(first, w[KV0:Q0, :], NT) + vectors[4:5, 0:384]
    for h in range(3):
        tile = kv[:, h * 128 : h * 128 + 128]
        kvb[place.chip, :, h * 128 : h * 128 + 128] = turn(tile, tab, h != 1, h == 1).astype(BF)
    gather = Gather(place, links, kvb, kv_view)
    gather.begin()
    low, high = lane_mask(True), lane_mask(False)
    qa = dot(first, w[Q0 : Q0 + 128, :], NT) + vectors[4:5, 384:512]
    qb = dot(first, w[Q0 + 64 : Q0 + 192, :], NT)
    qa = (turn(qa, tab, True, True)).astype(BF) * HD**-0.5
    qb = pltpu.roll(qb, 64, 1) + vectors[4:5, 512:640]
    qb = (turn(qb, tab, True, False)).astype(BF) * HD**-0.5
    zero = jnp.zeros((ROWS, 128), BF)
    q_o[0] = jnp.where(low, qa, zero)
    q_o[1] = jnp.where(high, qa, zero)
    q_o[2] = jnp.where(low, qb, zero)
    gather.first()
    gather.own_line()
    inner = dot(second, w[I0:U0, :]) + vectors[5:6]
    inner_o[...] = inner
    act = (inner * (0.5 * (1.0 + lax.erf(inner * (2.0**-0.5))))).astype(BF)
    gather.second()
    branch = dot(act, w[U0:SLAB, :])
    part[0] = branch[:, 0:384]
    part[1] = branch[:, 384:768]

    def scores(kk, h):
        keys = kvb[kk, :, h * 128 : h * 128 + 128]
        return keys, dot(keys, q_o[h], NT)

    causal = lax.broadcasted_iota(jnp.int32, (ROWS, ROWS), 0) <= lax.broadcasted_iota(
        jnp.int32, (ROWS, ROWS), 1
    )
    for h in range(3):
        keys, s = scores(place.chip, h)
        s = jnp.where(causal, s, -1e30)
        m = jnp.max(s, axis=0, keepdims=True)
        p = jnp.exp(s - m)
        top[h] = m
        total[h] = jnp.sum(p, axis=0, keepdims=True)
        acc[h] = dot(keys, p.astype(BF), TN)

    def step(n, carry):
        for j, action in (
            (0, lambda: gather.third(0)),
            (4, lambda: gather.third(-1)),
            (5, lambda: gather.third(1)),
            (8, lambda: gather.fourth(0)),
            (9, lambda: gather.third(2)),
            (10, lambda: gather.fourth(-1)),
            (12, lambda: gather.fourth(1)),
            (14, lambda: gather.fourth(2)),
        ):
            pl.when(n == j)(action)
        kk = place.slot(pick(n, [o[0] for o in ORDER_F]), pick(n, [o[1] for o in ORDER_F]))

        @pl.when(kk < place.chip)
        def _():
            for h in range(3):
                keys, s = scores(kk, h)
                old = top[h]
                m = jnp.maximum(old, jnp.max(s, axis=0, keepdims=True))
                p = jnp.exp(s - m)
                fade = jnp.exp(old - m)
                top[h] = m
                total[h] = total[h] * fade + jnp.sum(p, axis=0, keepdims=True)
                acc[h] = acc[h] * fade + dot(keys, p.astype(BF), TN)

        return carry

    lax.fori_loop(0, 15, step, 0)
    store = pltpu.make_async_copy(kvb, kv_o, local.at[1])
    store.start()
    heads = []
    for h in range(3):
        rows = slice(0, 64) if h == 1 else slice(64, 128)
        heads.append(acc[h, rows, :] / total[h])
        lse_o[h : h + 1, :] = top[h] + jnp.log(total[h])
    attn = jnp.concatenate([heads[1], heads[0], heads[2]], axis=0)
    ot_o[...] = attn
    branch = dot(attn.astype(BF), w[O0:I0, :], TN)
    part[0] = part[0] + branch[:, 0:384]
    part[1] = part[1] + branch[:, 384:768]
    mates_scatter(place, links, part, rounded, landing, "y")
    y = mates_scattered(place, links, part, rounded, landing, "y")
    y_ref[...] = (y + x_ref[...].astype(F32) + vectors[6:7, 0:384]).astype(BF)
    store.wait()
    links.finish()


def backward_kernel(
    l, g_ref, xg, slab, slab2, small, tab, tabt, kv, q, ot, lse, inner, *refs
):
    if l == 0:
        above, gx_ref, wg, sg, piece, *refs = refs
        *refs, above_v, a1, a2, b1, b2 = refs
    else:
        gx_ref, wg, sg, *refs = refs
    (w, gg, kvb, dkv, dqt, do, first, second, act, slope, part, rounded, landing,
     r1, r2, u1, u2, send_sems, recv_sems, local) = refs
    place = Place()
    links = Links(send_sems, recv_sems)
    load = load_layer(l, place, slab, slab2, w, local.at[0])
    load_kv = pltpu.make_async_copy(kv, kvb, local.at[1])
    load_kv.start()
    if l == 0:
        load_above = pltpu.make_async_copy(above, above_v, local.at[2])
        load_above.start()
    place.greet(mates=(1, 2))
    mates_gather(place, links, g_ref, gg, "g")
    if l == 0:
        load_above.wait()
        upper = Scatter(place, links, above_v, slab_view, a1, a2, b1, b2, "w")
        upper.begin()
    vectors = small[l].astype(F32)
    x = jnp.concatenate([xg[0], xg[1]], axis=1).astype(F32)
    normed, scale = normalize(x)
    first[...] = (normed * vectors[0:1] + vectors[2:3]).astype(BF)
    second[...] = (normed * vectors[1:2] + vectors[3:4]).astype(BF)
    value = inner[...]
    cdf = 0.5 * (1.0 + lax.erf(value * (2.0**-0.5)))
    act[...] = (value * cdf).astype(BF)
    slope[...] = cdf + value * jnp.exp(-0.5 * value * value) * 0.3989422804014327
    load.wait()
    mates_gathered(place, links, gg, "g")
    g = jnp.concatenate([gg[0], gg[1]], axis=1)
    low, high = lane_mask(True), lane_mask(False)
    zero = jnp.zeros((ROWS, 128), BF)
    da = dot(g, w[O0 : O0 + 128, :], NT).astype(BF)
    db = dot(g, w[O0 + 64 : O0 + 192, :], NT).astype(BF)
    do[0] = jnp.where(high, da, zero)
    do[1] = jnp.where(low, da, zero)
    do[2] = jnp.where(high, db, zero)
    dot_t = dot(w[O0:I0, :], g, NT).astype(BF).astype(F32) * ot[...]
    delta = [
        jnp.sum(dot_t[s : s + 64], axis=0, keepdims=True) for s in (64, 0, 128)
    ]
    if l == 0:
        upper.middle()
    load_kv.wait()
    dqt[...] = jnp.zeros_like(dqt)
    scatter = Scatter(place, links, dkv, kv_view, r1, r2, u1, u2)

    def chunk(kk, mask):
        for h in range(3):
            keys = kvb[kk, :, h * 128 : h * 128 + 128]
            p = jnp.exp(dot(keys, q[h], NT) - lse[h : h + 1, :])
            if mask is not None:
                p = jnp.where(mask, p, 0.0)
            dp = dot(keys, do[h], NT)
            ds = (p * (dp - delta[h])).astype(BF)
            dkv[kk, :, h * 128 : h * 128 + 128] = (dot(ds, q[h]) + dot(p.astype(BF), do[h])).astype(BF)
            dqt[h] = dqt[h] + dot(keys, ds, TN)

    def events(j):
        a, b = ORDER_B[j]
        if b == 2:
            for s in (1, -1):
                scatter.v1(0, s, a)
        if a == 2:
            for s in (1, -1):
                scatter.v1(1, s, b)
        if j == 7:
            for s in (1, -1):
                scatter.v2(0, s, 2)
                scatter.v2(1, s, 2)
        if j >= 7:
            if b in (1, -1):
                scatter.v2(0, b, a)
            if a in (1, -1):
                scatter.v2(1, a, b)

    def step(n, carry):
        kk = place.slot(pick(n, [o[0] for o in ORDER_B]), pick(n, [o[1] for o in ORDER_B]))

        @pl.when(kk < place.chip)
        def _():
            chunk(kk, None)

        @pl.when(kk > place.chip)
        def _():
            dkv[kk] = jnp.zeros((ROWS, 384), BF)

        for j in range(15):
            pl.when(n == j)(functools.partial(events, j))
        return carry

    lax.fori_loop(0, 15, step, 0)
    chunk(
        place.chip,
        lax.broadcasted_iota(jnp.int32, (ROWS, ROWS), 0)
        <= lax.broadcasted_iota(jnp.int32, (ROWS, ROWS), 1),
    )
    g = jnp.concatenate([gg[0], gg[1]], axis=1)
    grad_inner = (dot(g, w[U0:SLAB, :], NT) * slope[...]).astype(BF)
    wg[U0:SLAB, :] = dot(act[...], g, TN).astype(BF)
    if l == 0:
        upper.tail_one()
    scatter.tail_one()
    wg[I0:U0, :] = dot(second[...], grad_inner, TN).astype(BF)
    if l == 0:
        upper.tail_two()
    scatter.tail_two()
    grad_second = dot(grad_inner, w[I0:U0, :], NT)
    wg[O0:I0, :] = dot(ot[...].astype(BF), g).astype(BF)
    scatter.tail_three()
    if l == 0:
        upper.tail_three()
    sg[0:1, :] = jnp.sum(grad_second * normed, axis=0, keepdims=True)
    sg[1:2, :] = jnp.sum(grad_second, axis=0, keepdims=True)
    sg[2:3, :] = jnp.sum(grad_inner.astype(F32), axis=0, keepdims=True)
    sg[3:4, :] = jnp.sum(g.astype(F32), axis=0, keepdims=True)
    sg[6:8, :] = jnp.zeros((2, D), F32)
    rows = []
    for h in range(3):
        base = 64 if h == 1 else 0
        dq = dqt[h, base : base + 64, :] * HD**-0.5
        a, b = dq[0:8], dq[8:16]
        rows += [a * tabt[0] + b * tabt[1], b * tabt[0] - a * tabt[1], dq[16:64]]
    dq = jnp.concatenate(rows, axis=0).astype(BF)
    wg[Q0:O0, :] = dot(dq, first[...]).astype(BF)
    grad_first = dot(dq, w[Q0:O0, :], TN)
    q_sums = dot(jnp.ones((8, ROWS), BF), dq, NT)
    pre = jnp.concatenate([scatter.last(0), scatter.last(1)], axis=0)
    tiles = [
        turn(pre[:, h * 128 : h * 128 + 128], tab, h != 1, h == 1, -1.0).astype(BF)
        for h in range(3)
    ]
    pre = jnp.concatenate(tiles, axis=1)
    wg[KV0:Q0, :] = dot(pre, first[...], TN).astype(BF)
    grad_first = grad_first + dot(pre, w[KV0:Q0, :])
    sg[4:5, :] = jnp.sum(grad_first * normed, axis=0, keepdims=True)
    sg[5:6, :] = jnp.sum(grad_first, axis=0, keepdims=True)
    sg[6:7, 0:384] = jnp.sum(pre.astype(F32), axis=0, keepdims=True)
    sg[7:8, 0:192] = q_sums[0:1, :]
    grad_norm = grad_first * vectors[0:1] + grad_second * vectors[1:2]
    grad_x = scale * (
        grad_norm
        - jnp.mean(grad_norm, axis=-1, keepdims=True)
        - normed * jnp.mean(grad_norm * normed, axis=-1, keepdims=True)
    )
    part[0] = grad_x[:, 0:384]
    part[1] = grad_x[:, 384:768]
    mates_scatter(place, links, part, rounded, landing, "gx")
    if l == 0:
        for h in (0, 1):
            piece[:, h * 384 : h * 384 + 384] = upper.last(h)
    grad = mates_scattered(place, links, part, rounded, landing, "gx")
    gx_ref[...] = (grad + g_ref[...].astype(F32)).astype(BF)
    links.finish()


def grads_kernel(
    wg0, piece1, sg0, sg1, out, out_small, buf, own, piece, got, r1, r2, u1, u2,
    sm, along_x, along_z, across, beside, send_sems, recv_sems, local
):
    place = Place()
    links = Links(send_sems, recv_sems)
    load = pltpu.make_async_copy(wg0, own, local.at[0])
    load.start()
    place.greet(mates=(1, 2, 3), partner=True, far=True)
    sm[0, 0] = sg0[...]
    sm[0, 1] = sg1[...]
    for d in (1, 2, 3):
        links.send(("sx", d), lambda d=d: (sm.at[0], along_x.at[d - 1], place.at(d, 0)))

    def small_z():
        total = sm[0]
        for d in (1, 2, 3):
            links.arrived(("sx", d), along_x.at[d - 1], place.at(d, 0))
            total = total + along_x[d - 1]
        sm[1] = total
        for d in (1, 2, 3):
            links.send(("sz", d), lambda d=d: (sm.at[1], along_z.at[d - 1], place.at(0, d)))

    def small_pipe():
        total = sm[1]
        for d in (1, 2, 3):
            links.arrived(("sz", d), along_z.at[d - 1], place.at(0, d))
            total = total + along_z[d - 1]
        sm[2] = total
        links.send("sp", lambda: (sm.at[2, 1 - place.pipe], across, place.partner()))

    def small_mates():
        links.arrived("sp", across, place.partner())
        sm[3, 0] = sm[2, place.pipe] + across[...]
        for r in (1, 2, 3):
            links.send(("sm", r), lambda r=r: (sm.at[3, 0], beside.at[r - 1], place.mate(r)[2]))

    def small_last():
        total = sm[3, 0]
        for r in (1, 2, 3):
            links.arrived(("sm", r), beside.at[r - 1], place.mate(r)[2])
            total = total + beside[r - 1]
        row = lax.broadcasted_iota(jnp.int32, (8, D), 0)
        norm = (row < 2) | ((row >= 4) & (row < 6))
        out_small[place.core] = jnp.where(norm, total, sm[3, 0])
        out_small[1 - place.core] = jnp.where(norm, total, beside[0])

    load.wait()
    scatter = Scatter(place, links, own, slab_view, r1, r2, u1, u2)
    scatter.begin()
    small_z()
    scatter.middle()
    small_pipe()
    scatter.tail_one()
    scatter.tail_two()
    scatter.tail_three()
    small_mates()
    device = place.partner()
    lower_pipe = place.pipe == 0
    for h in (0, 1):
        lanes = pl.ds(h * 384, 384)
        zero, one = scatter.last(h), piece1[:, lanes]
        piece[:, lanes] = jnp.where(lower_pipe, zero, one)
        got[0, :, lanes] = jnp.where(lower_pipe, one, zero).astype(BF)
    for i, (base, rows) in enumerate(PARTS):
        span = pl.ds(base, rows)
        links.send(("piece", i), lambda span=span: (got.at[0, span], got.at[1, span], device))

    def whole(i):
        span = pl.ds(*PARTS[i])
        links.arrived(("piece", i), got.at[1, span], device)
        buf[place.core, place.chip, span] = (piece[span] + got[1, span].astype(F32)).astype(BF)

    sibling = place.mate(1)[2]

    def pass_on(a, b):
        ref = lambda: buf.at[place.core, place.slot(a, b)]
        links.send(("core", a, b), lambda: (ref(), ref(), sibling))

    parts = [Gather(place, links, buf.at[place.core], part_view(i), i) for i in range(2)]
    gather_parts(parts, whole, pass_on)
    keep = pltpu.make_async_copy(buf.at[place.core], out.at[place.core], local.at[0])
    keep.start()
    small_last()
    for a, b in ((0, 0), *ORDER_F):
        links.arrived(("core", a, b), buf.at[1 - place.core, place.slot(a, b)], sibling)
    rest = pltpu.make_async_copy(buf.at[1 - place.core], out.at[1 - place.core], local.at[1])
    rest.start()
    keep.wait()
    rest.wait()
    links.finish()


VMEM = pl.BlockSpec(memory_space=pltpu.VMEM)
ANY = pl.BlockSpec(memory_space=pl.ANY)


def sems(n, m):
    return [pltpu.SemaphoreType.DMA((n,)), pltpu.SemaphoreType.DMA((n,)), pltpu.SemaphoreType.DMA((m,))]


def shape(dims, kind=BF):
    return jax.ShapeDtypeStruct(dims, kind)


def params(i):
    return pltpu.CompilerParams(collective_id=i, has_side_effects=True, vmem_limit_bytes=56 * 2**20)


def share_weights(*args):
    return pl.pallas_call(
        weights_kernel,
        name="share_weights",
        out_shape=(shape((SLAB, D)), shape((CHIPS, PIECE, D)), shape((2, 16, D))),
        in_specs=[ANY, ANY, ANY, ANY, VMEM, VMEM, VMEM, VMEM, VMEM],
        out_specs=(ANY, ANY, VMEM),
        scratch_shapes=[
            pltpu.VMEM((SLAB, D), BF),
            pltpu.VMEM((CHIPS, PIECE, D), BF),
            pltpu.VMEM((3, D, 384), BF),
            pltpu.VMEM((384, D), BF),
            pltpu.VMEM((16, D), F32),
            pltpu.VMEM((2, 16, D), BF),
            *sems(96, 8),
        ],
        compiler_params=params(0),
    )(*args)


def forward(l, x, slab, small, tab):
    return pl.pallas_call(
        functools.partial(forward_kernel, l),
        name=f"layer_{l}_forward",
        out_shape=(
            shape((128, 384)),
            shape((2, ROWS, 384)),
            shape((CHIPS, ROWS, 384)),
            shape((3, ROWS, 128)),
            shape((192, ROWS), F32),
            shape((8, ROWS), F32),
            shape((ROWS, D), F32),
        ),
        in_specs=[VMEM, ANY, ANY, VMEM, VMEM],
        out_specs=(VMEM, VMEM, ANY, VMEM, VMEM, VMEM, VMEM),
        scratch_shapes=[
            pltpu.VMEM((SLAB, D), BF),
            pltpu.VMEM((2, ROWS, 384), BF),
            pltpu.VMEM((CHIPS, ROWS, 384), BF),
            pltpu.VMEM((3, 128, ROWS), F32),
            pltpu.VMEM((3, 1, ROWS), F32),
            pltpu.VMEM((3, 1, ROWS), F32),
            pltpu.VMEM((2, ROWS, 384), F32),
            pltpu.VMEM((2, ROWS, 384), BF),
            pltpu.VMEM((3, 128, 384), BF),
            *sems(48, 2),
        ],
        compiler_params=params(1 + l),
    )(x, *slab, small, tab)


def landing_shapes(rows, part):
    return [
        pltpu.VMEM((2, 2, 4, part, 384), BF),
        pltpu.VMEM((2, 2, 4, rows, 384), BF),
        pltpu.VMEM((2, 2, part, 384), BF),
        pltpu.VMEM((2, 2, rows, 384), BF),
    ]


def backward(l, g, kept, slab, small, tab, tabt, above=()):
    xg, kv, q, ot, lse, inner = kept
    extra = [VMEM] if l == 0 else []
    return pl.pallas_call(
        functools.partial(backward_kernel, l),
        name=f"layer_{l}_backward",
        out_shape=(
            shape((128, 384)),
            shape((SLAB, D)),
            shape((8, D), F32),
            *([shape((PIECE, D), F32)] if l == 0 else []),
        ),
        in_specs=[VMEM, VMEM, ANY, ANY, VMEM, VMEM, VMEM, ANY, VMEM, VMEM, VMEM, VMEM, *([ANY] if l == 0 else [])],
        out_specs=(VMEM, VMEM, VMEM, *extra),
        scratch_shapes=[
            pltpu.VMEM((SLAB, D), BF),
            pltpu.VMEM((2, ROWS, 384), BF),
            pltpu.VMEM((CHIPS, ROWS, 384), BF),
            pltpu.VMEM((CHIPS, ROWS, 384), BF),
            pltpu.VMEM((3, 128, ROWS), F32),
            pltpu.VMEM((3, ROWS, 128), BF),
            pltpu.VMEM((ROWS, D), BF),
            pltpu.VMEM((ROWS, D), BF),
            pltpu.VMEM((ROWS, D), BF),
            pltpu.VMEM((ROWS, D), F32),
            pltpu.VMEM((2, ROWS, 384), F32),
            pltpu.VMEM((2, ROWS, 384), BF),
            pltpu.VMEM((3, 128, 384), BF),
            *landing_shapes(128, 64),
            *sems(96, 3),
            *([pltpu.VMEM((CHIPS, PIECE, D), BF), *landing_shapes(PIECE, 80)] if l == 0 else []),
        ],
        compiler_params=params(3 + l),
    )(g, xg, *slab, small, tab, tabt, kv, q, ot, lse, inner, *above)


def share_grads(*args):
    return pl.pallas_call(
        grads_kernel,
        name="share_grads",
        out_shape=(shape((2, CHIPS, PIECE, D)), shape((2, 8, D), F32)),
        in_specs=[ANY, VMEM, VMEM, VMEM],
        out_specs=(ANY, VMEM),
        scratch_shapes=[
            pltpu.VMEM((2, CHIPS, PIECE, D), BF),
            pltpu.VMEM((CHIPS, PIECE, D), BF),
            pltpu.VMEM((PIECE, D), F32),
            pltpu.VMEM((2, PIECE, D), BF),
            *landing_shapes(PIECE, 80),
            pltpu.VMEM((4, 2, 8, D), F32),
            pltpu.VMEM((3, 2, 8, D), F32),
            pltpu.VMEM((3, 2, 8, D), F32),
            pltpu.VMEM((8, D), F32),
            pltpu.VMEM((3, 8, D), F32),
            *sems(176, 2),
        ],
        compiler_params=params(5),
    )(*args)


def finish_kernel(
    whole, small, g_qkv, g_out, g_in, g_down, g_gain, g_shift, g_qkv_b, g_out_b, g_in_b,
    held, qkv, out, wide, down, local,
):
    regions = ((U0, SLAB), (I0, U0), (O0, I0), (KV0, O0))
    loads = []
    for i, (lo, hi) in enumerate(regions):
        for c in (0, 1):
            rows = pl.ds(lo, hi - lo)
            load = pltpu.make_async_copy(whole.at[c, rows], held.at[c, rows], local.at[2 * i + c])
            load.start()
            loads.append(load)
    tensor = lax.axis_index("tensor")
    rows = [small[0], small[1]]

    def features(row):
        return jnp.where(tensor == 0, row[:, 0:384], row[:, 384:768])

    g_gain[0:1] = features(rows[0][4:5])
    g_gain[1:2] = features(rows[0][0:1])
    g_shift[0:1] = features(rows[0][5:6])
    g_shift[1:2] = features(rows[0][1:2])
    g_out_b[...] = features(rows[0][3:4])
    g_in_b[...] = jnp.concatenate([rows[0][2:3], rows[1][2:3]], axis=1)
    for j in range(3):
        pieces = []
        for c in (0, 1):
            for i in [BLOCKS.index((j, h)) for h in range(3)]:
                row, at = (6, i) if i < 6 else (7, i - 6)
                pieces.append(rows[c][row : row + 1, at * 64 : at * 64 + 64])
        g_qkv_b[j : j + 1] = jnp.concatenate(pieces, axis=1)
    stores = []

    def store(i, src, dst):
        copy = pltpu.make_async_copy(src, dst, local.at[8 + i])
        copy.start()
        stores.append(copy)

    for c in (0, 1):
        loads[c].wait()
        down[c * 768 : c * 768 + 768] = held[c, U0:SLAB].astype(F32)
        store(c, down.at[pl.ds(c * 768, 768)], g_down.at[pl.ds(c * 768, 768)])
    for c in (0, 1):
        loads[2 + c].wait()
        wide[:, c * 768 : c * 768 + 768] = held[c, I0:U0].astype(F32)
    store(2, wide, g_in)
    for c in (0, 1):
        loads[4 + c].wait()
        for i, block in enumerate((1, 0, 2)):
            start = c * 192 + block * 64
            out[start : start + 64] = held[c, O0 + i * 64 : O0 + i * 64 + 64].astype(F32)
    store(3, out, g_out)
    for c in (0, 1):
        loads[6 + c].wait()
    for j in range(3):
        pieces = []
        for c in (0, 1):
            for i in [BLOCKS.index((j, h)) for h in range(3)]:
                pieces.append(held[c, i * 64 : i * 64 + 64])
        qkv[j] = jnp.concatenate(pieces, axis=0).astype(F32).T
        store(4 + j, qkv.at[j], g_qkv.at[j])
    for copy in stores:
        copy.wait()


def finish(whole, small):
    return pl.pallas_call(
        finish_kernel,
        name="finish",
        out_shape=(
            shape((3, D, 384), F32),
            shape((384, D), F32),
            shape((D, 1536), F32),
            shape((1536, D), F32),
            shape((2, 384), F32),
            shape((2, 384), F32),
            shape((3, 384), F32),
            shape((1, 384), F32),
            shape((1, 1536), F32),
        ),
        in_specs=[ANY, VMEM],
        out_specs=(ANY, ANY, ANY, ANY, VMEM, VMEM, VMEM, VMEM, VMEM),
        scratch_shapes=[
            pltpu.VMEM((2, SLAB, D), BF),
            pltpu.VMEM((3, D, 384), F32),
            pltpu.VMEM((384, D), F32),
            pltpu.VMEM((D, 1536), F32),
            pltpu.VMEM((1536, D), F32),
            pltpu.SemaphoreType.DMA((16,)),
        ],
        compiler_params=pltpu.CompilerParams(vmem_limit_bytes=56 * 2**20),
    )(whole, small)


def rope_tables(chip):
    half = HD // 8
    freqs = 10000.0 ** (-2.0 * jnp.arange(half, dtype=F32) / (2 * half))
    positions = chip * ROWS + jnp.arange(ROWS, dtype=jnp.int32)
    angles = positions.astype(F32)[:, None] * freqs[None, :]
    cosine, sine = jnp.cos(angles), jnp.sin(angles)
    none = jnp.zeros((ROWS, half), F32)
    rest = jnp.zeros((ROWS, HD - 2 * half), F32)
    tiles = [
        jnp.concatenate([cosine, cosine, rest + 1.0], axis=1),
        jnp.concatenate([none, sine, rest], axis=1),
        jnp.concatenate([-sine, none, rest], axis=1),
    ]
    tab = jnp.stack([jnp.concatenate([tile, tile], axis=1) for tile in tiles])
    return tab, jnp.stack([cosine.T, sine.T])


def body(
    inputs, cotangent, ln_gain, ln_bias, qkv_weight, qkv_bias, out_weight, out_bias,
    fc_in_weight, fc_in_bias, fc_out_weight,
):
    pipe = lax.axis_index("pipe")
    ctx = lax.axis_index("ctx")
    tab, tabt = rope_tables(ctx // 2)
    mine, theirs, smalls = share_weights(
        qkv_weight[0], out_weight[0], fc_in_weight[0], fc_out_weight[0], ln_gain[0], ln_bias[0],
        qkv_bias[0], fc_in_bias, out_bias,
    )
    slabs = mine, theirs.reshape(SLAB, D)

    x = lax.dynamic_index_in_dim(inputs, pipe, 0, keepdims=False)
    g = lax.dynamic_index_in_dim(cotangent, pipe, 0, keepdims=False)
    middle, *kept0 = forward(0, x, slabs, smalls, tab)
    upper, *kept1 = forward(1, middle, slabs, smalls, tab)
    g, wg1, sg1 = backward(1, g, kept1, slabs, smalls, tab, tabt)
    above = wg1.reshape(CHIPS, PIECE, D)
    g, wg0, sg0, piece1 = backward(0, g, kept0, slabs, smalls, tab, tabt, (above,))

    lower_pipe = pipe == 0
    sent = jnp.where(lower_pipe, upper, g)
    held = jnp.where(lower_pipe, g, upper)
    got = lax.ppermute(sent, "pipe", [(0, 1), (1, 0)])
    boundary = jnp.stack([jnp.where(lower_pipe, held, got), jnp.where(lower_pipe, got, held)])[None]

    whole, sums = share_grads(
        wg0.reshape(CHIPS, PIECE, D), piece1, sg0, sg1
    )
    g_qkv, g_out, g_in, g_down, g_gain, g_shift, g_qkv_b, g_out_b, g_in_b = finish(
        whole.reshape(2, SLAB, D), sums
    )
    return (
        boundary,
        g_gain[None],
        g_shift[None],
        g_qkv[None],
        g_qkv_b[None],
        g_out[None],
        g_out_b,
        g_in[None],
        g_in_b,
        g_down[None],
    )


def solution(mesh):
    return jax.shard_map(
        body,
        mesh=mesh,
        in_specs=(
            P(None, "ctx", "tensor"),
            P(None, "ctx", "tensor"),
            P("pipe", None, None),
            P("pipe", None, None),
            P("pipe", None, None, "tensor"),
            P("pipe", None, "tensor"),
            P("pipe", "tensor", None),
            P("pipe", "tensor"),
            P("pipe", None, "tensor"),
            P("pipe", "tensor"),
            P("pipe", "tensor", None),
        ),
        out_specs=(
            P("pipe", None, "ctx", "tensor"),
            P("pipe", None, "tensor"),
            P("pipe", None, "tensor"),
            P("pipe", None, None, "tensor"),
            P("pipe", None, "tensor"),
            P("pipe", "tensor", None),
            P("pipe", "tensor"),
            P("pipe", None, "tensor"),
            P("pipe", "tensor"),
            P("pipe", "tensor", None),
        ),
        check_vma=False,
    )
```

```python
import functools

import jax
import jax.numpy as jnp
from jax import lax
from jax.experimental import pallas as pl
from jax.experimental.pallas import tpu as pltpu
from jax.sharding import PartitionSpec as P


D = 768
HD = 64
F32 = jnp.float32
BF = jnp.bfloat16
MESH = pl.DeviceIdType.MESH
EPS = 1e-05
CHIPS = 16
ROWS = 256
PIECE = 144
SLAB = CHIPS * PIECE
KV0, Q0, O0, I0, U0 = 0, 384, 576, 768, 1536
BLOCKS = ((1, 0), (2, 0), (2, 1), (1, 1), (1, 2), (2, 2), (0, 0), (0, 1), (0, 2))
NN = (((1,), (0,)), ((), ()))
NT = (((1,), (1,)), ((), ()))
TN = (((0,), (0,)), ((), ()))


def dot(a, b, dims=NN):
    return lax.dot_general(a, b, dims, preferred_element_type=F32)


class Place:
    def __init__(self):
        self.pipe = lax.axis_index("pipe")
        self.tensor = lax.axis_index("tensor")
        ctx = lax.axis_index("ctx")
        self.core = lax.rem(ctx, 2)
        self.chip = ctx // 2
        self.x = self.chip // 4
        self.z = lax.rem(self.chip, 4)

    def slot(self, dx, dz):
        return lax.rem(self.x + (dx + 4), 4) * 4 + lax.rem(self.z + (dz + 4), 4)

    def at(self, dx, dz):
        return (self.pipe, self.tensor, self.slot(dx, dz) * 2 + self.core)

    def mate(self, r):
        t = lax.rem(self.tensor + r // 2, 2)
        c = lax.rem(self.core + r % 2, 2)
        return t, c, (self.pipe, t, self.chip * 2 + c)

    def partner(self):
        return (1 - self.pipe, self.tensor, self.chip * 2 + self.core)

    def greet(self, mates=(), partner=False, far=False):
        bar = pltpu.get_barrier_semaphore()
        targets = [self.at(1, 0), self.at(-1, 0), self.at(0, 1), self.at(0, -1)]
        if far:
            targets += [self.at(2, 0), self.at(0, 2)]
        targets += [self.mate(r)[2] for r in mates]
        if partner:
            targets.append(self.partner())
        for target in targets:
            pl.semaphore_signal(bar, inc=1, device_id=target, device_id_type=MESH)
        pl.semaphore_wait(bar, len(targets))


class Links:
    def __init__(self, send_sems, recv_sems):
        self.send_sems, self.recv_sems = send_sems, recv_sems
        self.ids, self.sent = {}, []

    def desc(self, key, src, dst, device):
        i = self.ids.setdefault(key, len(self.ids))
        return pltpu.make_async_remote_copy(
            src_ref=src,
            dst_ref=dst,
            send_sem=self.send_sems.at[i],
            recv_sem=self.recv_sems.at[i],
            device_id=device,
            device_id_type=MESH,
        )

    def send(self, key, copy):
        self.desc(key, *copy()).start()
        self.sent.append((key, copy))

    def arrived(self, key, dst, device):
        self.desc(key, dst, dst, device).wait_recv()

    def finish(self):
        for key, copy in self.sent:
            self.desc(key, *copy()).wait_send()


def kv_view(h, part):
    start, size = {"all": (0, 128), 0: (0, 64), 1: (64, 64)}[part]
    return (pl.ds(h * 128 + start, size), pl.ds(0, 384))


def slab_view(h, part, base=0, rows=PIECE):
    cut = (rows // 2 + 8) // 16 * 16
    cut = rows - cut if h else cut
    start, size = {"all": (0, rows), 0: (0, cut), 1: (cut, rows - cut)}[part]
    return (pl.ds(base + start, size), pl.ds(h * 384, 384))


PARTS = ((0, 80), (80, 64))


def part_view(i):
    return lambda h, part: slab_view(h, part, *PARTS[i])


class Gather:
    def __init__(self, place, links, buf, view, tag=""):
        self.place, self.links, self.buf, self.view, self.tag = place, links, buf, view, tag

    def ref(self, du, dv, h, part):
        slot = self.place.slot(du, dv) if h == 0 else self.place.slot(dv, du)
        return self.buf.at[(slot,) + self.view(h, part)]

    def dev(self, along_u, step, h):
        return self.place.at(step, 0) if along_u == (h == 0) else self.place.at(0, step)

    def snd(self, h, along_u, step, du, dv, part):
        key = (self.tag, h, along_u, step, du - (step if along_u else 0), dv - (0 if along_u else step), part)
        ref = lambda: self.ref(du, dv, h, part)
        self.links.send(key, lambda: (ref(), ref(), self.dev(along_u, step, h)))

    def rcv(self, h, along_u, step, du, dv, part):
        key = (self.tag, h, along_u, step, du, dv, part)
        self.links.arrived(key, self.ref(du, dv, h, part), self.dev(along_u, step, h))

    def begin(self):
        for h in (0, 1):
            for step in (1, -1):
                self.snd(h, True, step, 0, 0, "all")

    def own_line(self):
        for h in (0, 1):
            for step in (1, -1):
                self.snd(h, False, step, 0, 0, "all")

    def first(self):
        for h in (0, 1):
            for step, part in ((1, 0), (-1, 1)):
                self.rcv(h, True, step, -step, 0, "all")
                self.snd(h, True, step, -step, 0, part)
                for s in (1, -1):
                    self.snd(h, False, s, -step, 0, "all")

    def second(self):
        for h in (0, 1):
            for step, part in ((1, 0), (-1, 1)):
                self.rcv(h, True, step, -2 * step, 0, part)
            for s in (1, -1):
                self.snd(h, False, s, 2, 0, "all")

    def third(self, du):
        for h in (0, 1):
            for step, part in ((1, 0), (-1, 1)):
                self.rcv(h, False, step, du, -step, "all")
                self.snd(h, False, step, du, -step, part)

    def fourth(self, du):
        for h in (0, 1):
            for step, part in ((1, 0), (-1, 1)):
                self.rcv(h, False, step, du, -2 * step, part)


def gather_parts(parts, arrived, done=lambda a, b: None):
    for i, part in enumerate(parts):
        arrived(i)
        part.begin()
    done(0, 0)
    for part in parts:
        part.first()
        part.own_line()
    for part in parts:
        part.second()
    for stage, du, slots in (
        ("third", 0, ORDER_F[0:4]),
        ("third", -1, ORDER_F[4:5]),
        ("third", 1, ORDER_F[5:8]),
        ("third", 2, ()),
        ("fourth", 0, ORDER_F[8:10]),
        ("fourth", -1, ORDER_F[10:12]),
        ("fourth", 1, ORDER_F[12:14]),
        ("fourth", 2, ORDER_F[14:15]),
    ):
        for part in parts:
            getattr(part, stage)(du)
        for a, b in slots:
            done(a, b)


class Scatter:
    def __init__(self, place, links, buf, view, r1, r2, u1, u2, tag=""):
        self.place, self.links, self.buf, self.view = place, links, buf, view
        self.r1, self.r2, self.u1, self.u2, self.tag = r1, r2, u1, u2, tag

    def ref(self, du, dv, h, part):
        slot = self.place.slot(du, dv) if h == 0 else self.place.slot(dv, du)
        return self.buf.at[(slot,) + self.view(h, part)]

    def dev(self, along_u, step, h):
        return self.place.at(step, 0) if along_u == (h == 0) else self.place.at(0, step)

    def size(self, h, part):
        return pl.ds(0, self.view(h, part)[0].size)

    def land(self, stage, h, step, du):
        d, e = (step + 1) // 2, (du + 4) % 4
        part = (1 - d) if stage in ("v1", "u1") else "all"
        rows = self.size(h, part)
        return {
            "v1": lambda: self.r1.at[h, d, e, rows],
            "v2": lambda: self.r2.at[h, d, e, rows],
            "u1": lambda: self.u1.at[h, d, rows],
            "u2": lambda: self.u2.at[h, d, rows],
        }[stage]()

    def snd(self, stage, h, step, du, src):
        key = (self.tag, stage, h, step, du)
        device = lambda: self.dev(stage[0] == "u", step, h)
        self.links.send(key, lambda: (src(), self.land(stage, h, step, du), device()))

    def rcv(self, stage, h, step, du):
        ref = self.land(stage, h, step, du)
        self.links.arrived((self.tag, stage, h, step, du), ref, self.dev(stage[0] == "u", step, h))
        return ref

    def v1(self, h, step, du):
        self.snd("v1", h, step, du, lambda: self.ref(du, 2, h, (1 - step) // 2))

    def v2(self, h, step, du):
        got = self.rcv("v1", h, step, du)
        mine = self.ref(du, step, h, (1 - step) // 2)
        mine[...] = (mine[...].astype(F32) + got[...].astype(F32)).astype(BF)
        self.snd("v2", h, step, du, lambda: self.ref(du, step, h, "all"))

    def vsum(self, h, du):
        one, two = self.rcv("v2", h, 1, du), self.rcv("v2", h, -1, du)
        mine = self.ref(du, 0, h, "all")
        mine[...] = (mine[...].astype(F32) + one[...].astype(F32) + two[...].astype(F32)).astype(BF)

    def u1s(self, h):
        for step in (1, -1):
            self.snd("u1", h, step, 0, lambda step=step: self.ref(2, 0, h, (1 - step) // 2))

    def u2s(self, h, step):
        got = self.rcv("u1", h, step, 0)
        mine = self.ref(step, 0, h, (1 - step) // 2)
        mine[...] = (mine[...].astype(F32) + got[...].astype(F32)).astype(BF)
        self.snd("u2", h, step, 0, lambda: self.ref(step, 0, h, "all"))

    def last(self, h):
        one, two = self.rcv("u2", h, 1, 0), self.rcv("u2", h, -1, 0)
        mine = self.ref(0, 0, h, "all")
        return mine[...].astype(F32) + one[...].astype(F32) + two[...].astype(F32)

    def begin(self):
        for du in (2, -1, 1, 0):
            for h in (0, 1):
                for step in (1, -1):
                    self.v1(h, step, du)

    def middle(self):
        for du in (2, -1, 1, 0):
            for h in (0, 1):
                for step in (1, -1):
                    self.v2(h, step, du)

    def tail_one(self):
        for h in (0, 1):
            self.vsum(h, 2)
            self.u1s(h)

    def tail_two(self):
        for h in (0, 1):
            for step in (1, -1):
                self.vsum(h, step)
                self.u2s(h, step)

    def tail_three(self):
        for h in (0, 1):
            self.vsum(h, 0)


def pick(n, values):
    out = 0
    for j, v in enumerate(values):
        out = out + (n == j).astype(jnp.int32) * v
    return out


def mates_gather(place, links, own, full, tag):
    rows = pl.ds(pl.multiple_of(place.core * 128, 128), 128)
    for r in (2, 1):
        device = place.mate(r)[2]
        links.send((tag, r), lambda device=device: (own, full.at[place.tensor, rows], device))
    full[place.tensor, rows] = own[...]


def mates_gathered(place, links, full, tag):
    rows = pl.ds(pl.multiple_of(place.core * 128, 128), 128)
    others = pl.ds(pl.multiple_of(128 - place.core * 128, 128), 128)
    far, sibling = place.mate(2)[2], place.mate(1)[2]
    links.arrived((tag, 2), full.at[1 - place.tensor, rows], far)
    passed = full.at[1 - place.tensor, rows]
    links.send((tag, 3), lambda: (passed, passed, sibling))
    links.arrived((tag, 1), full.at[place.tensor, others], sibling)
    links.arrived((tag, 3), full.at[1 - place.tensor, others], sibling)


def mates_scatter(place, links, part, rounded, landing, tag):
    others = pl.ds(pl.multiple_of(128 - place.core * 128, 128), 128)
    rounded[:, others] = part[:, others].astype(BF)
    device = place.mate(1)[2]
    links.send((tag, 1), lambda: (rounded.at[:, others], landing.at[pl.ds(0, 2)], device))


def mates_scattered(place, links, part, rounded, landing, tag):
    rows = pl.ds(pl.multiple_of(place.core * 128, 128), 128)
    links.arrived((tag, 1), landing.at[pl.ds(0, 2)], place.mate(1)[2])
    away = part[1 - place.tensor, rows] + landing[1 - place.tensor].astype(F32)
    rounded[1 - place.tensor, rows] = away.astype(BF)
    device = place.mate(2)[2]
    links.send((tag, 2), lambda: (rounded.at[1 - place.tensor, rows], landing.at[2], device))
    total = part[place.tensor, rows] + landing[place.tensor].astype(F32)
    links.arrived((tag, 2), landing.at[2], device)
    return total + landing[2].astype(F32)


def normalize(values):
    centered = values - jnp.mean(values, axis=-1, keepdims=True)
    variance = jnp.mean(centered * centered, axis=-1, keepdims=True)
    scale = lax.rsqrt(variance + EPS)
    return centered * scale, scale


def lane_mask(lower, shape=(ROWS, 128)):
    lane = lax.broadcasted_iota(jnp.int32, shape, 1)
    return lane < 64 if lower else lane >= 64


def turn(values, tab, lower, upper, sign=1.0):
    cosine, plus, minus = tab[0], tab[1], tab[2]
    turned = (
        values * cosine
        + sign * (pltpu.roll(values, 8, 1) * plus + pltpu.roll(values, 120, 1) * minus)
    )
    if lower and upper:
        return turned
    return jnp.where(lane_mask(lower), turned, values)


def weights_kernel(
    qkv, out, fc_in, fc_out, gain, shift, qkv_b, in_b, out_b, mine, theirs, all_small,
    own, buf, raw, turned, small, got_small, send_sems, recv_sems, local,
):
    place = Place()
    links = Links(send_sems, recv_sems)
    core = place.core
    loads = [pltpu.make_async_copy(qkv, raw, local.at[0])]
    for i, block in enumerate((1, 0, 2)):
        rows = pl.ds(pl.multiple_of(core * 192 + block * 64, 64), 64)
        loads.append(pltpu.make_async_copy(out.at[rows], own.at[pl.ds(O0 + i * 64, 64)], local.at[1 + i]))
    half = pl.ds(pl.multiple_of(core * 768, 768), 768)
    loads.append(pltpu.make_async_copy(fc_in.at[:, half], own.at[pl.ds(I0, 768)], local.at[4]))
    loads.append(pltpu.make_async_copy(fc_out.at[half], own.at[pl.ds(U0, 768)], local.at[5]))
    for load in loads:
        load.start()
    place.greet(partner=True)
    small[...] = jnp.zeros_like(small)
    small[0:2] = gain[...].astype(F32)
    small[2:4] = shift[...].astype(F32)
    bias = qkv_b[...].astype(F32)
    bias = jnp.where(core == 0, bias[:, 0:192], bias[:, 192:384])
    pieces = [bias[j : j + 1, h * 64 : h * 64 + 64] for j, h in BLOCKS]
    small[4:5, 0:576] = jnp.concatenate(pieces, axis=1)
    wide = in_b[...].astype(F32)
    small[5:6] = jnp.where(core == 0, wide[:, 0:768], wide[:, 768:1536])
    small[6:7, 0:384] = out_b[...].astype(F32)
    rounded = small[...].astype(BF)
    all_small[place.pipe] = rounded
    loads[0].wait()
    for j in range(3):
        turned[...] = raw[j].T
        for i, (k, h) in enumerate(BLOCKS):
            if k == j:
                own[i * 64 : i * 64 + 64, :] = turned[pl.ds(pl.multiple_of(core * 192 + h * 64, 64), 64), :]
    for load in loads[1:]:
        load.wait()
    device = place.partner()
    for i, (base, rows) in enumerate(PARTS):
        src = own.at[pl.ds(pl.multiple_of(place.chip * PIECE + base, 16), rows)]
        dst = buf.at[place.chip, pl.ds(base, rows)]
        links.send(("slab", i), lambda src=src, dst=dst: (src, dst, device))
    got_small[0] = rounded
    links.send("small", lambda: (got_small.at[0], got_small.at[1], device))
    keep = pltpu.make_async_copy(own, mine, local.at[6])
    keep.start()

    def piece(i):
        links.arrived(("slab", i), buf.at[place.chip, pl.ds(*PARTS[i])], device)

    gather_parts([Gather(place, links, buf, part_view(i), i) for i in range(2)], piece)
    store = pltpu.make_async_copy(buf, theirs, local.at[7])
    store.start()
    links.arrived("small", got_small.at[1], device)
    all_small[1 - place.pipe] = got_small[1]
    keep.wait()
    store.wait()
    links.finish()


def load_layer(l, place, mine, theirs, w, sem):
    pl.when(place.pipe == l)(lambda: pltpu.make_async_copy(mine, w, sem).start())
    pl.when(place.pipe != l)(lambda: pltpu.make_async_copy(theirs, w, sem).start())
    return pltpu.make_async_copy(mine, w, sem)


ORDER_F = ((0, -1), (0, 1), (-1, 0), (1, 0), (-1, -1), (-1, 1), (1, -1), (1, 1), (0, 2), (2, 0), (-1, 2), (2, -1), (1, 2), (2, 1), (2, 2))
ORDER_B = ((2, 2), (0, 2), (2, 0), (-1, 2), (1, 2), (2, -1), (2, 1), (-1, -1), (-1, 1), (1, -1), (1, 1), (0, -1), (0, 1), (-1, 0), (1, 0))


def forward_part(
    l, place, links, load, x_ref, small, tab, y_ref, xg, kvb, q_o, ot_o, lse_o, inner_o,
    w, acc, top, total, part, rounded, landing,
):
    mates_gather(place, links, x_ref, xg, ("x", l))
    vectors = small[l].astype(F32)
    mates_gathered(place, links, xg, ("x", l))
    x = jnp.concatenate([xg[0], xg[1]], axis=1).astype(F32)
    normed, _ = normalize(x)
    first = (normed * vectors[0:1] + vectors[2:3]).astype(BF)
    second = (normed * vectors[1:2] + vectors[3:4]).astype(BF)
    load.wait()
    kv = dot(first, w[KV0:Q0, :], NT) + vectors[4:5, 0:384]
    for h in range(3):
        tile = kv[:, h * 128 : h * 128 + 128]
        kvb[place.chip, :, h * 128 : h * 128 + 128] = turn(tile, tab, h != 1, h == 1).astype(BF)
    gather = Gather(place, links, kvb, kv_view, ("kv", l))
    gather.begin()
    low, high = lane_mask(True), lane_mask(False)
    qa = dot(first, w[Q0 : Q0 + 128, :], NT) + vectors[4:5, 384:512]
    qb = dot(first, w[Q0 + 64 : Q0 + 192, :], NT)
    qa = (turn(qa, tab, True, True)).astype(BF) * HD**-0.5
    qb = pltpu.roll(qb, 64, 1) + vectors[4:5, 512:640]
    qb = (turn(qb, tab, True, False)).astype(BF) * HD**-0.5
    zero = jnp.zeros((ROWS, 128), BF)
    q_o[0] = jnp.where(low, qa, zero)
    q_o[1] = jnp.where(high, qa, zero)
    q_o[2] = jnp.where(low, qb, zero)
    gather.first()
    gather.own_line()
    inner = dot(second, w[I0:U0, :]) + vectors[5:6]
    inner_o[...] = inner
    act = (inner * (0.5 * (1.0 + lax.erf(inner * (2.0**-0.5))))).astype(BF)
    gather.second()
    branch = dot(act, w[U0:SLAB, :])
    part[0] = branch[:, 0:384]
    part[1] = branch[:, 384:768]

    def scores(kk, h):
        keys = kvb[kk, :, h * 128 : h * 128 + 128]
        return keys, dot(keys, q_o[h], NT)

    causal = lax.broadcasted_iota(jnp.int32, (ROWS, ROWS), 0) <= lax.broadcasted_iota(
        jnp.int32, (ROWS, ROWS), 1
    )
    for h in range(3):
        keys, s = scores(place.chip, h)
        s = jnp.where(causal, s, -1e30)
        m = jnp.max(s, axis=0, keepdims=True)
        p = jnp.exp(s - m)
        top[h] = m
        total[h] = jnp.sum(p, axis=0, keepdims=True)
        acc[h] = dot(keys, p.astype(BF), TN)

    def step(n, carry):
        for j, action in (
            (0, lambda: gather.third(0)),
            (2, lambda: gather.third(-1)),
            (4, lambda: gather.third(1)),
            (6, lambda: gather.third(2)),
            (8, lambda: gather.fourth(0)),
            (10, lambda: gather.fourth(-1)),
            (12, lambda: gather.fourth(1)),
            (14, lambda: gather.fourth(2)),
        ):
            pl.when(n == j)(action)
        kk = place.slot(pick(n, [o[0] for o in ORDER_F]), pick(n, [o[1] for o in ORDER_F]))

        @pl.when(kk < place.chip)
        def _():
            for h in range(3):
                keys, s = scores(kk, h)
                old = top[h]
                m = jnp.maximum(old, jnp.max(s, axis=0, keepdims=True))
                p = jnp.exp(s - m)
                fade = jnp.exp(old - m)
                top[h] = m
                total[h] = total[h] * fade + jnp.sum(p, axis=0, keepdims=True)
                acc[h] = acc[h] * fade + dot(keys, p.astype(BF), TN)

        return carry

    lax.fori_loop(0, 15, step, 0)
    heads = []
    for h in range(3):
        rows = slice(0, 64) if h == 1 else slice(64, 128)
        heads.append(acc[h, rows, :] / total[h])
        lse_o[h : h + 1, :] = top[h] + jnp.log(total[h])
    attn = jnp.concatenate([heads[1], heads[0], heads[2]], axis=0)
    ot_o[...] = attn
    branch = dot(attn.astype(BF), w[O0:I0, :], TN)
    part[0] = part[0] + branch[:, 0:384]
    part[1] = part[1] + branch[:, 384:768]
    mates_scatter(place, links, part, rounded, landing, ("y", l))
    y = mates_scattered(place, links, part, rounded, landing, ("y", l))
    y_ref[...] = (y + x_ref[...].astype(F32) + vectors[6:7, 0:384]).astype(BF)


def backward_part(
    l, place, links, g_ref, xg, small, tab, tabt, kvb, q, ot, lse, inner, gx_ref, wg, sg,
    w, gg, dkv, dqt, do, first, second, act, slope, part, rounded, landing, r1, r2, u1, u2,
    upper=None, piece=None,
):
    mates_gather(place, links, g_ref, gg, ("g", l))
    if upper is not None:
        upper.begin()
    vectors = small[l].astype(F32)
    x = jnp.concatenate([xg[0], xg[1]], axis=1).astype(F32)
    normed, scale = normalize(x)
    first[...] = (normed * vectors[0:1] + vectors[2:3]).astype(BF)
    second[...] = (normed * vectors[1:2] + vectors[3:4]).astype(BF)
    value = inner[...]
    cdf = 0.5 * (1.0 + lax.erf(value * (2.0**-0.5)))
    act[...] = (value * cdf).astype(BF)
    slope[...] = cdf + value * jnp.exp(-0.5 * value * value) * 0.3989422804014327
    mates_gathered(place, links, gg, ("g", l))
    g = jnp.concatenate([gg[0], gg[1]], axis=1)
    low, high = lane_mask(True), lane_mask(False)
    zero = jnp.zeros((ROWS, 128), BF)
    da = dot(g, w[O0 : O0 + 128, :], NT).astype(BF)
    db = dot(g, w[O0 + 64 : O0 + 192, :], NT).astype(BF)
    do[0] = jnp.where(high, da, zero)
    do[1] = jnp.where(low, da, zero)
    do[2] = jnp.where(high, db, zero)
    dot_t = dot(w[O0:I0, :], g, NT).astype(BF).astype(F32) * ot[...]
    delta = [
        jnp.sum(dot_t[s : s + 64], axis=0, keepdims=True) for s in (64, 0, 128)
    ]
    if upper is not None:
        upper.middle()
    dqt[...] = jnp.zeros_like(dqt)
    scatter = Scatter(place, links, dkv, kv_view, r1, r2, u1, u2, ("d", l))

    def chunk(kk, mask):
        for h in range(3):
            keys = kvb[kk, :, h * 128 : h * 128 + 128]
            p = jnp.exp(dot(keys, q[h], NT) - lse[h : h + 1, :])
            if mask is not None:
                p = jnp.where(mask, p, 0.0)
            dp = dot(keys, do[h], NT)
            ds = (p * (dp - delta[h])).astype(BF)
            dkv[kk, :, h * 128 : h * 128 + 128] = (dot(ds, q[h]) + dot(p.astype(BF), do[h])).astype(BF)
            dqt[h] = dqt[h] + dot(keys, ds, TN)

    def events(j):
        a, b = ORDER_B[j]
        if b == 2:
            for s in (1, -1):
                scatter.v1(0, s, a)
        if a == 2:
            for s in (1, -1):
                scatter.v1(1, s, b)
        if j == 7:
            for s in (1, -1):
                scatter.v2(0, s, 2)
                scatter.v2(1, s, 2)
        if j >= 7:
            if b in (1, -1):
                scatter.v2(0, b, a)
            if a in (1, -1):
                scatter.v2(1, a, b)

    def step(n, carry):
        kk = place.slot(pick(n, [o[0] for o in ORDER_B]), pick(n, [o[1] for o in ORDER_B]))

        @pl.when(kk < place.chip)
        def _():
            chunk(kk, None)

        @pl.when(kk > place.chip)
        def _():
            dkv[kk] = jnp.zeros((ROWS, 384), BF)

        for j in range(15):
            pl.when(n == j)(functools.partial(events, j))
        return carry

    lax.fori_loop(0, 15, step, 0)
    chunk(
        place.chip,
        lax.broadcasted_iota(jnp.int32, (ROWS, ROWS), 0)
        <= lax.broadcasted_iota(jnp.int32, (ROWS, ROWS), 1),
    )
    g = jnp.concatenate([gg[0], gg[1]], axis=1)
    grad_inner = (dot(g, w[U0:SLAB, :], NT) * slope[...]).astype(BF)
    wg[U0:SLAB, :] = dot(act[...], g, TN).astype(BF)
    if upper is not None:
        upper.tail_one()
    scatter.tail_one()
    wg[I0:U0, :] = dot(second[...], grad_inner, TN).astype(BF)
    if upper is not None:
        upper.tail_two()
    scatter.tail_two()
    grad_second = dot(grad_inner, w[I0:U0, :], NT)
    wg[O0:I0, :] = dot(ot[...].astype(BF), g).astype(BF)
    scatter.tail_three()
    if upper is not None:
        upper.tail_three()
    sg[0:1, :] = jnp.sum(grad_second * normed, axis=0, keepdims=True)
    sg[1:2, :] = jnp.sum(grad_second, axis=0, keepdims=True)
    sg[2:3, :] = jnp.sum(grad_inner.astype(F32), axis=0, keepdims=True)
    sg[3:4, :] = jnp.sum(g.astype(F32), axis=0, keepdims=True)
    sg[6:8, :] = jnp.zeros((2, D), F32)
    rows = []
    for h in range(3):
        base = 64 if h == 1 else 0
        dq = dqt[h, base : base + 64, :] * HD**-0.5
        a, b = dq[0:8], dq[8:16]
        rows += [a * tabt[0] + b * tabt[1], b * tabt[0] - a * tabt[1], dq[16:64]]
    dq = jnp.concatenate(rows, axis=0).astype(BF)
    wg[Q0:O0, :] = dot(dq, first[...]).astype(BF)
    grad_first = dot(dq, w[Q0:O0, :], TN)
    q_sums = dot(jnp.ones((8, ROWS), BF), dq, NT)
    pre = jnp.concatenate([scatter.last(0), scatter.last(1)], axis=0)
    tiles = [
        turn(pre[:, h * 128 : h * 128 + 128], tab, h != 1, h == 1, -1.0).astype(BF)
        for h in range(3)
    ]
    pre = jnp.concatenate(tiles, axis=1)
    wg[KV0:Q0, :] = dot(pre, first[...], TN).astype(BF)
    grad_first = grad_first + dot(pre, w[KV0:Q0, :])
    sg[4:5, :] = jnp.sum(grad_first * normed, axis=0, keepdims=True)
    sg[5:6, :] = jnp.sum(grad_first, axis=0, keepdims=True)
    sg[6:7, 0:384] = jnp.sum(pre.astype(F32), axis=0, keepdims=True)
    sg[7:8, 0:192] = q_sums[0:1, :]
    grad_norm = grad_first * vectors[0:1] + grad_second * vectors[1:2]
    grad_x = scale * (
        grad_norm
        - jnp.mean(grad_norm, axis=-1, keepdims=True)
        - normed * jnp.mean(grad_norm * normed, axis=-1, keepdims=True)
    )
    part[0] = grad_x[:, 0:384]
    part[1] = grad_x[:, 384:768]
    mates_scatter(place, links, part, rounded, landing, ("gx", l))
    if upper is not None:
        for h in (0, 1):
            piece[:, h * 384 : h * 384 + 384] = upper.last(h)
    grad = mates_scattered(place, links, part, rounded, landing, ("gx", l))
    gx_ref[...] = (grad + g_ref[...].astype(F32)).astype(BF)


class Rows:
    def __init__(self, ref):
        self.ref = ref

    def __setitem__(self, index, value):
        start, stop = index[0].start, index[0].stop
        for row in range(start, stop, 48):
            self.ref[row // PIECE, row % PIECE : row % PIECE + 48, :] = value[row - start : row - start + 48]


def layers_kernel(
    x_ref, g_ref, slab, slab2, small, tab, tabt, y_ref, gx_ref, wg0, sg0, sg1, piece,
    w, middle, xg, kvb, q, ot, lse, inner, acc, top, total, part, rounded, landing,
    g_mid, gg, dkv, do, first, second, act, slope, r1, r2, u1, u2, wg1, a1, a2, b1, b2,
    send_sems, recv_sems, local,
):
    place = Place()
    links = Links(send_sems, recv_sems)
    loads = [load_layer(l, place, slab, slab2, w.at[l], local.at[l]) for l in (0, 1)]
    place.greet(mates=(1, 2))
    for l, (entry, exit_ref) in enumerate(((x_ref, middle), (middle, y_ref))):
        forward_part(
            l, place, links, loads[l], entry, small, tab, exit_ref, xg.at[l], kvb.at[l], q.at[l],
            ot.at[l], lse.at[l], inner.at[l], w.at[l], acc, top, total, part, rounded.at[l],
            landing.at[l],
        )
    for l, entry, exit_ref, wg, sg in ((1, g_ref, g_mid, wg1, sg1), (0, g_mid, gx_ref, wg0, sg0)):
        upper = Scatter(place, links, wg1, slab_view, a1, a2, b1, b2, "w") if l == 0 else None
        backward_part(
            l, place, links, entry, xg.at[l], small, tab, tabt, kvb.at[l], q.at[l], ot.at[l],
            lse.at[l], inner.at[l], exit_ref, Rows(wg), sg, w.at[l], gg.at[l], dkv.at[l], acc, do,
            first, second, act, slope, part, rounded.at[2 + l], landing.at[2 + l],
            r1.at[l], r2.at[l], u1.at[l], u2.at[l], upper, piece,
        )
    links.finish()


def grads_kernel(
    wg0, piece1, sg0, sg1, out, out_small, buf, own, piece, got, r1, r2, u1, u2,
    sm, along_x, along_z, across, beside, send_sems, recv_sems, local
):
    place = Place()
    links = Links(send_sems, recv_sems)
    load = pltpu.make_async_copy(wg0, own, local.at[0])
    load.start()
    place.greet(mates=(1, 2, 3), partner=True, far=True)
    sm[0, 0] = sg0[...]
    sm[0, 1] = sg1[...]
    for d in (1, 2, 3):
        links.send(("sx", d), lambda d=d: (sm.at[0], along_x.at[d - 1], place.at(d, 0)))

    def small_z():
        total = sm[0]
        for d in (1, 2, 3):
            links.arrived(("sx", d), along_x.at[d - 1], place.at(d, 0))
            total = total + along_x[d - 1]
        sm[1] = total
        for d in (1, 2, 3):
            links.send(("sz", d), lambda d=d: (sm.at[1], along_z.at[d - 1], place.at(0, d)))

    def small_pipe():
        total = sm[1]
        for d in (1, 2, 3):
            links.arrived(("sz", d), along_z.at[d - 1], place.at(0, d))
            total = total + along_z[d - 1]
        sm[2] = total
        links.send("sp", lambda: (sm.at[2, 1 - place.pipe], across, place.partner()))

    def small_mates():
        links.arrived("sp", across, place.partner())
        sm[3, 0] = sm[2, place.pipe] + across[...]
        for r in (1, 2, 3):
            links.send(("sm", r), lambda r=r: (sm.at[3, 0], beside.at[r - 1], place.mate(r)[2]))

    def small_last():
        total = sm[3, 0]
        for r in (1, 2, 3):
            links.arrived(("sm", r), beside.at[r - 1], place.mate(r)[2])
            total = total + beside[r - 1]
        row = lax.broadcasted_iota(jnp.int32, (8, D), 0)
        norm = (row < 2) | ((row >= 4) & (row < 6))
        out_small[place.core] = jnp.where(norm, total, sm[3, 0])
        out_small[1 - place.core] = jnp.where(norm, total, beside[0])

    load.wait()
    scatter = Scatter(place, links, own, slab_view, r1, r2, u1, u2)
    scatter.begin()
    small_z()
    scatter.middle()
    small_pipe()
    scatter.tail_one()
    scatter.tail_two()
    scatter.tail_three()
    small_mates()
    device = place.partner()
    lower_pipe = place.pipe == 0
    for h in (0, 1):
        lanes = pl.ds(h * 384, 384)
        zero, one = scatter.last(h), piece1[:, lanes]
        piece[:, lanes] = jnp.where(lower_pipe, zero, one)
        got[0, :, lanes] = jnp.where(lower_pipe, one, zero).astype(BF)
    for i, (base, rows) in enumerate(PARTS):
        span = pl.ds(base, rows)
        links.send(("piece", i), lambda span=span: (got.at[0, span], got.at[1, span], device))

    def whole(i):
        span = pl.ds(*PARTS[i])
        links.arrived(("piece", i), got.at[1, span], device)
        buf[place.core, place.chip, span] = (piece[span] + got[1, span].astype(F32)).astype(BF)

    sibling = place.mate(1)[2]

    def pass_on(a, b):
        ref = lambda: buf.at[place.core, place.slot(a, b)]
        links.send(("core", a, b), lambda: (ref(), ref(), sibling))

    parts = [Gather(place, links, buf.at[place.core], part_view(i), i) for i in range(2)]
    gather_parts(parts, whole, pass_on)
    keep = pltpu.make_async_copy(buf.at[place.core], out.at[place.core], local.at[0])
    keep.start()
    small_last()
    for a, b in ((0, 0), *ORDER_F):
        links.arrived(("core", a, b), buf.at[1 - place.core, place.slot(a, b)], sibling)
    rest = pltpu.make_async_copy(buf.at[1 - place.core], out.at[1 - place.core], local.at[1])
    rest.start()
    keep.wait()
    rest.wait()
    links.finish()


VMEM = pl.BlockSpec(memory_space=pltpu.VMEM)
ANY = pl.BlockSpec(memory_space=pl.ANY)


def sems(n, m):
    return [pltpu.SemaphoreType.DMA((n,)), pltpu.SemaphoreType.DMA((n,)), pltpu.SemaphoreType.DMA((m,))]


def shape(dims, kind=BF):
    return jax.ShapeDtypeStruct(dims, kind)


def params(i):
    return pltpu.CompilerParams(collective_id=i, has_side_effects=True, vmem_limit_bytes=56 * 2**20)


def share_weights(*args):
    return pl.pallas_call(
        weights_kernel,
        name="share_weights",
        out_shape=(shape((SLAB, D)), shape((CHIPS, PIECE, D)), shape((2, 16, D))),
        in_specs=[ANY, ANY, ANY, ANY, VMEM, VMEM, VMEM, VMEM, VMEM],
        out_specs=(ANY, ANY, VMEM),
        scratch_shapes=[
            pltpu.VMEM((SLAB, D), BF),
            pltpu.VMEM((CHIPS, PIECE, D), BF),
            pltpu.VMEM((3, D, 384), BF),
            pltpu.VMEM((384, D), BF),
            pltpu.VMEM((16, D), F32),
            pltpu.VMEM((2, 16, D), BF),
            *sems(96, 8),
        ],
        compiler_params=params(0),
    )(*args)


def landing_shapes(rows, part, lead=()):
    return [
        pltpu.VMEM((*lead, 2, 2, 4, part, 384), BF),
        pltpu.VMEM((*lead, 2, 2, 4, rows, 384), BF),
        pltpu.VMEM((*lead, 2, 2, part, 384), BF),
        pltpu.VMEM((*lead, 2, 2, rows, 384), BF),
    ]


def layers(*args):
    def pair(dims, kind=BF, n=2):
        return pltpu.VMEM((n, *dims), kind)

    return pl.pallas_call(
        layers_kernel,
        name="layers",
        out_shape=(
            shape((128, 384)),
            shape((128, 384)),
            shape((CHIPS, PIECE, D)),
            shape((8, D), F32),
            shape((8, D), F32),
            shape((PIECE, D), F32),
        ),
        in_specs=[VMEM, VMEM, ANY, ANY, VMEM, VMEM, VMEM],
        out_specs=(VMEM,) * 6,
        scratch_shapes=[
            pair((SLAB, D)),
            pltpu.VMEM((128, 384), BF),
            pair((2, ROWS, 384)),
            pair((CHIPS, ROWS, 384)),
            pair((3, ROWS, 128)),
            pair((192, ROWS), F32),
            pair((8, ROWS), F32),
            pair((ROWS, D), F32),
            pltpu.VMEM((3, 128, ROWS), F32),
            pltpu.VMEM((3, 1, ROWS), F32),
            pltpu.VMEM((3, 1, ROWS), F32),
            pltpu.VMEM((2, ROWS, 384), F32),
            pair((2, ROWS, 384), n=4),
            pair((3, 128, 384), n=4),
            pltpu.VMEM((128, 384), BF),
            pair((2, ROWS, 384)),
            pair((CHIPS, ROWS, 384)),
            pltpu.VMEM((3, ROWS, 128), BF),
            pltpu.VMEM((ROWS, D), BF),
            pltpu.VMEM((ROWS, D), BF),
            pltpu.VMEM((ROWS, D), BF),
            pltpu.VMEM((ROWS, D), F32),
            *landing_shapes(128, 64, (2,)),
            pltpu.VMEM((CHIPS, PIECE, D), BF),
            *landing_shapes(PIECE, 80),
            *sems(232, 2),
        ],
        compiler_params=params(1),
    )(*args)


def share_grads(*args):
    return pl.pallas_call(
        grads_kernel,
        name="share_grads",
        out_shape=(shape((2, CHIPS, PIECE, D)), shape((2, 8, D), F32)),
        in_specs=[ANY, VMEM, VMEM, VMEM],
        out_specs=(ANY, VMEM),
        scratch_shapes=[
            pltpu.VMEM((2, CHIPS, PIECE, D), BF),
            pltpu.VMEM((CHIPS, PIECE, D), BF),
            pltpu.VMEM((PIECE, D), F32),
            pltpu.VMEM((2, PIECE, D), BF),
            *landing_shapes(PIECE, 80),
            pltpu.VMEM((4, 2, 8, D), F32),
            pltpu.VMEM((3, 2, 8, D), F32),
            pltpu.VMEM((3, 2, 8, D), F32),
            pltpu.VMEM((8, D), F32),
            pltpu.VMEM((3, 8, D), F32),
            *sems(176, 2),
        ],
        compiler_params=params(5),
    )(*args)


def finish_kernel(
    whole, small, g_qkv, g_out, g_in, g_down, g_gain, g_shift, g_qkv_b, g_out_b, g_in_b,
    held, qkv, out, wide, down, local,
):
    regions = ((U0, SLAB), (I0, U0), (O0, I0), (KV0, O0))
    loads = []
    for i, (lo, hi) in enumerate(regions):
        for c in (0, 1):
            rows = pl.ds(lo, hi - lo)
            load = pltpu.make_async_copy(whole.at[c, rows], held.at[c, rows], local.at[2 * i + c])
            load.start()
            loads.append(load)
    tensor = lax.axis_index("tensor")
    rows = [small[0], small[1]]

    def features(row):
        return jnp.where(tensor == 0, row[:, 0:384], row[:, 384:768])

    g_gain[0:1] = features(rows[0][4:5])
    g_gain[1:2] = features(rows[0][0:1])
    g_shift[0:1] = features(rows[0][5:6])
    g_shift[1:2] = features(rows[0][1:2])
    g_out_b[...] = features(rows[0][3:4])
    g_in_b[...] = jnp.concatenate([rows[0][2:3], rows[1][2:3]], axis=1)
    for j in range(3):
        pieces = []
        for c in (0, 1):
            for i in [BLOCKS.index((j, h)) for h in range(3)]:
                row, at = (6, i) if i < 6 else (7, i - 6)
                pieces.append(rows[c][row : row + 1, at * 64 : at * 64 + 64])
        g_qkv_b[j : j + 1] = jnp.concatenate(pieces, axis=1)
    stores = []

    def store(i, src, dst):
        copy = pltpu.make_async_copy(src, dst, local.at[8 + i])
        copy.start()
        stores.append(copy)

    for c in (0, 1):
        loads[c].wait()
        down[c * 768 : c * 768 + 768] = held[c, U0:SLAB].astype(F32)
        store(c, down.at[pl.ds(c * 768, 768)], g_down.at[pl.ds(c * 768, 768)])
    for c in (0, 1):
        loads[2 + c].wait()
        wide[:, c * 768 : c * 768 + 768] = held[c, I0:U0].astype(F32)
    store(2, wide, g_in)
    for c in (0, 1):
        loads[4 + c].wait()
        for i, block in enumerate((1, 0, 2)):
            start = c * 192 + block * 64
            out[start : start + 64] = held[c, O0 + i * 64 : O0 + i * 64 + 64].astype(F32)
    store(3, out, g_out)
    for c in (0, 1):
        loads[6 + c].wait()
    for j in range(3):
        pieces = []
        for c in (0, 1):
            for i in [BLOCKS.index((j, h)) for h in range(3)]:
                pieces.append(held[c, i * 64 : i * 64 + 64])
        qkv[j] = jnp.concatenate(pieces, axis=0).astype(F32).T
        store(4 + j, qkv.at[j], g_qkv.at[j])
    for copy in stores:
        copy.wait()


def finish(whole, small):
    return pl.pallas_call(
        finish_kernel,
        name="finish",
        out_shape=(
            shape((3, D, 384), F32),
            shape((384, D), F32),
            shape((D, 1536), F32),
            shape((1536, D), F32),
            shape((2, 384), F32),
            shape((2, 384), F32),
            shape((3, 384), F32),
            shape((1, 384), F32),
            shape((1, 1536), F32),
        ),
        in_specs=[ANY, VMEM],
        out_specs=(ANY, ANY, ANY, ANY, VMEM, VMEM, VMEM, VMEM, VMEM),
        scratch_shapes=[
            pltpu.VMEM((2, SLAB, D), BF),
            pltpu.VMEM((3, D, 384), F32),
            pltpu.VMEM((384, D), F32),
            pltpu.VMEM((D, 1536), F32),
            pltpu.VMEM((1536, D), F32),
            pltpu.SemaphoreType.DMA((16,)),
        ],
        compiler_params=pltpu.CompilerParams(vmem_limit_bytes=56 * 2**20),
    )(whole, small)


def rope_tables(chip):
    half = HD // 8
    freqs = 10000.0 ** (-2.0 * jnp.arange(half, dtype=F32) / (2 * half))
    positions = chip * ROWS + jnp.arange(ROWS, dtype=jnp.int32)
    angles = positions.astype(F32)[:, None] * freqs[None, :]
    cosine, sine = jnp.cos(angles), jnp.sin(angles)
    none = jnp.zeros((ROWS, half), F32)
    rest = jnp.zeros((ROWS, HD - 2 * half), F32)
    tiles = [
        jnp.concatenate([cosine, cosine, rest + 1.0], axis=1),
        jnp.concatenate([none, sine, rest], axis=1),
        jnp.concatenate([-sine, none, rest], axis=1),
    ]
    tab = jnp.stack([jnp.concatenate([tile, tile], axis=1) for tile in tiles])
    return tab, jnp.stack([cosine.T, sine.T])


def body(
    inputs, cotangent, ln_gain, ln_bias, qkv_weight, qkv_bias, out_weight, out_bias,
    fc_in_weight, fc_in_bias, fc_out_weight,
):
    pipe = lax.axis_index("pipe")
    ctx = lax.axis_index("ctx")
    tab, tabt = rope_tables(ctx // 2)
    mine, theirs, smalls = share_weights(
        qkv_weight[0], out_weight[0], fc_in_weight[0], fc_out_weight[0], ln_gain[0], ln_bias[0],
        qkv_bias[0], fc_in_bias, out_bias,
    )
    slabs = mine, theirs.reshape(SLAB, D)

    x = lax.dynamic_index_in_dim(inputs, pipe, 0, keepdims=False)
    g = lax.dynamic_index_in_dim(cotangent, pipe, 0, keepdims=False)
    upper, g, wg0, sg0, sg1, piece1 = layers(x, g, *slabs, smalls, tab, tabt)

    lower_pipe = pipe == 0
    sent = jnp.where(lower_pipe, upper, g)
    held = jnp.where(lower_pipe, g, upper)
    got = lax.ppermute(sent, "pipe", [(0, 1), (1, 0)])
    boundary = jnp.stack([jnp.where(lower_pipe, held, got), jnp.where(lower_pipe, got, held)])[None]

    whole, sums = share_grads(
        wg0, piece1, sg0, sg1
    )
    g_qkv, g_out, g_in, g_down, g_gain, g_shift, g_qkv_b, g_out_b, g_in_b = finish(
        whole.reshape(2, SLAB, D), sums
    )
    return (
        boundary,
        g_gain[None],
        g_shift[None],
        g_qkv[None],
        g_qkv_b[None],
        g_out[None],
        g_out_b,
        g_in[None],
        g_in_b,
        g_down[None],
    )


def solution(mesh):
    return jax.shard_map(
        body,
        mesh=mesh,
        in_specs=(
            P(None, "ctx", "tensor"),
            P(None, "ctx", "tensor"),
            P("pipe", None, None),
            P("pipe", None, None),
            P("pipe", None, None, "tensor"),
            P("pipe", None, "tensor"),
            P("pipe", "tensor", None),
            P("pipe", "tensor"),
            P("pipe", None, "tensor"),
            P("pipe", "tensor"),
            P("pipe", "tensor", None),
        ),
        out_specs=(
            P("pipe", None, "ctx", "tensor"),
            P("pipe", None, "tensor"),
            P("pipe", None, "tensor"),
            P("pipe", None, None, "tensor"),
            P("pipe", None, "tensor"),
            P("pipe", "tensor", None),
            P("pipe", "tensor"),
            P("pipe", None, "tensor"),
            P("pipe", "tensor"),
            P("pipe", "tensor", None),
        ),
        check_vma=False,
    )
```

```python
import functools

import jax
import jax.numpy as jnp
from jax import lax
from jax.experimental import pallas as pl
from jax.experimental.pallas import tpu as pltpu
from jax.sharding import PartitionSpec as P


D = 768
HD = 64
F32 = jnp.float32
BF = jnp.bfloat16
MESH = pl.DeviceIdType.MESH
EPS = 1e-05
CHIPS = 16
ROWS = 256
PIECE = 144
SLAB = CHIPS * PIECE
KV0, Q0, O0, I0, U0 = 0, 384, 576, 768, 1536
BLOCKS = ((1, 0), (2, 0), (2, 1), (1, 1), (1, 2), (2, 2), (0, 0), (0, 1), (0, 2))
NN = (((1,), (0,)), ((), ()))
NT = (((1,), (1,)), ((), ()))
TN = (((0,), (0,)), ((), ()))


def dot(a, b, dims=NN):
    return lax.dot_general(a, b, dims, preferred_element_type=F32)


class Place:
    def __init__(self):
        self.pipe = lax.axis_index("pipe")
        self.tensor = lax.axis_index("tensor")
        ctx = lax.axis_index("ctx")
        self.core = lax.rem(ctx, 2)
        self.chip = ctx // 2
        self.x = self.chip // 4
        self.z = lax.rem(self.chip, 4)

    def slot(self, dx, dz):
        return lax.rem(self.x + (dx + 4), 4) * 4 + lax.rem(self.z + (dz + 4), 4)

    def at(self, dx, dz):
        return (self.pipe, self.tensor, self.slot(dx, dz) * 2 + self.core)

    def mate(self, r):
        t = lax.rem(self.tensor + r // 2, 2)
        c = lax.rem(self.core + r % 2, 2)
        return t, c, (self.pipe, t, self.chip * 2 + c)

    def partner(self):
        return (1 - self.pipe, self.tensor, self.chip * 2 + self.core)

    def greet(self, mates=(), partner=False, far=False):
        bar = pltpu.get_barrier_semaphore()
        targets = [self.at(1, 0), self.at(-1, 0), self.at(0, 1), self.at(0, -1)]
        if far:
            targets += [self.at(2, 0), self.at(0, 2)]
        targets += [self.mate(r)[2] for r in mates]
        if partner:
            targets.append(self.partner())
        for target in targets:
            pl.semaphore_signal(bar, inc=1, device_id=target, device_id_type=MESH)
        pl.semaphore_wait(bar, len(targets))


class Links:
    def __init__(self, send_sems, recv_sems):
        self.send_sems, self.recv_sems = send_sems, recv_sems
        self.ids, self.sent = {}, []

    def desc(self, key, src, dst, device):
        i = self.ids.setdefault(key, len(self.ids))
        return pltpu.make_async_remote_copy(
            src_ref=src,
            dst_ref=dst,
            send_sem=self.send_sems.at[i],
            recv_sem=self.recv_sems.at[i],
            device_id=device,
            device_id_type=MESH,
        )

    def send(self, key, copy):
        self.desc(key, *copy()).start()
        self.sent.append((key, copy))

    def arrived(self, key, dst, device):
        self.desc(key, dst, dst, device).wait_recv()

    def finish(self):
        for key, copy in self.sent:
            self.desc(key, *copy()).wait_send()


def kv_view(h, part):
    start, size = {"all": (0, 128), 0: (0, 64), 1: (64, 64)}[part]
    return (pl.ds(h * 128 + start, size), pl.ds(0, 384))


def slab_view(h, part, base=0, rows=PIECE):
    cut = (rows // 2 + 8) // 16 * 16
    cut = rows - cut if h else cut
    start, size = {"all": (0, rows), 0: (0, cut), 1: (cut, rows - cut)}[part]
    return (pl.ds(base + start, size), pl.ds(h * 384, 384))


PARTS = ((0, 80), (80, 64))


def part_view(i):
    return lambda h, part: slab_view(h, part, *PARTS[i])


class Gather:
    def __init__(self, place, links, buf, view, tag=""):
        self.place, self.links, self.buf, self.view, self.tag = place, links, buf, view, tag

    def ref(self, du, dv, h, part):
        slot = self.place.slot(du, dv) if h == 0 else self.place.slot(dv, du)
        return self.buf.at[(slot,) + self.view(h, part)]

    def dev(self, along_u, step, h):
        return self.place.at(step, 0) if along_u == (h == 0) else self.place.at(0, step)

    def snd(self, h, along_u, step, du, dv, part):
        key = (self.tag, h, along_u, step, du - (step if along_u else 0), dv - (0 if along_u else step), part)
        ref = lambda: self.ref(du, dv, h, part)
        self.links.send(key, lambda: (ref(), ref(), self.dev(along_u, step, h)))

    def rcv(self, h, along_u, step, du, dv, part):
        key = (self.tag, h, along_u, step, du, dv, part)
        self.links.arrived(key, self.ref(du, dv, h, part), self.dev(along_u, step, h))

    def begin(self):
        for h in (0, 1):
            for step in (1, -1):
                self.snd(h, True, step, 0, 0, "all")

    def own_line(self):
        for h in (0, 1):
            for step in (1, -1):
                self.snd(h, False, step, 0, 0, "all")

    def first(self):
        for h in (0, 1):
            for step, part in ((1, 0), (-1, 1)):
                self.rcv(h, True, step, -step, 0, "all")
                self.snd(h, True, step, -step, 0, part)
                for s in (1, -1):
                    self.snd(h, False, s, -step, 0, "all")

    def second(self):
        for h in (0, 1):
            for step, part in ((1, 0), (-1, 1)):
                self.rcv(h, True, step, -2 * step, 0, part)
            for s in (1, -1):
                self.snd(h, False, s, 2, 0, "all")

    def third(self, du):
        for h in (0, 1):
            for step, part in ((1, 0), (-1, 1)):
                self.rcv(h, False, step, du, -step, "all")
                self.snd(h, False, step, du, -step, part)

    def fourth(self, du):
        for h in (0, 1):
            for step, part in ((1, 0), (-1, 1)):
                self.rcv(h, False, step, du, -2 * step, part)


def gather_parts(parts, arrived, done=lambda a, b: None):
    for i, part in enumerate(parts):
        arrived(i)
        part.begin()
    done(0, 0)
    for part in parts:
        part.first()
        part.own_line()
    for part in parts:
        part.second()
    for stage, du, slots in (
        ("third", 0, ORDER_F[0:4]),
        ("third", -1, ORDER_F[4:5]),
        ("third", 1, ORDER_F[5:8]),
        ("third", 2, ()),
        ("fourth", 0, ORDER_F[8:10]),
        ("fourth", -1, ORDER_F[10:12]),
        ("fourth", 1, ORDER_F[12:14]),
        ("fourth", 2, ORDER_F[14:15]),
    ):
        for part in parts:
            getattr(part, stage)(du)
        for a, b in slots:
            done(a, b)


class Scatter:
    def __init__(self, place, links, buf, view, r1, r2, u1, u2, tag=""):
        self.place, self.links, self.buf, self.view = place, links, buf, view
        self.r1, self.r2, self.u1, self.u2, self.tag = r1, r2, u1, u2, tag

    def ref(self, du, dv, h, part):
        slot = self.place.slot(du, dv) if h == 0 else self.place.slot(dv, du)
        return self.buf.at[(slot,) + self.view(h, part)]

    def dev(self, along_u, step, h):
        return self.place.at(step, 0) if along_u == (h == 0) else self.place.at(0, step)

    def size(self, h, part):
        return pl.ds(0, self.view(h, part)[0].size)

    def land(self, stage, h, step, du):
        d, e = (step + 1) // 2, (du + 4) % 4
        part = (1 - d) if stage in ("v1", "u1") else "all"
        rows = self.size(h, part)
        return {
            "v1": lambda: self.r1.at[h, d, e, rows],
            "v2": lambda: self.r2.at[h, d, e, rows],
            "u1": lambda: self.u1.at[h, d, rows],
            "u2": lambda: self.u2.at[h, d, rows],
        }[stage]()

    def snd(self, stage, h, step, du, src):
        key = (self.tag, stage, h, step, du)
        device = lambda: self.dev(stage[0] == "u", step, h)
        self.links.send(key, lambda: (src(), self.land(stage, h, step, du), device()))

    def rcv(self, stage, h, step, du):
        ref = self.land(stage, h, step, du)
        self.links.arrived((self.tag, stage, h, step, du), ref, self.dev(stage[0] == "u", step, h))
        return ref

    def v1(self, h, step, du):
        self.snd("v1", h, step, du, lambda: self.ref(du, 2, h, (1 - step) // 2))

    def v2(self, h, step, du):
        got = self.rcv("v1", h, step, du)
        mine = self.ref(du, step, h, (1 - step) // 2)
        mine[...] = (mine[...].astype(F32) + got[...].astype(F32)).astype(BF)
        self.snd("v2", h, step, du, lambda: self.ref(du, step, h, "all"))

    def vsum(self, h, du):
        one, two = self.rcv("v2", h, 1, du), self.rcv("v2", h, -1, du)
        mine = self.ref(du, 0, h, "all")
        mine[...] = (mine[...].astype(F32) + one[...].astype(F32) + two[...].astype(F32)).astype(BF)

    def u1s(self, h):
        for step in (1, -1):
            self.snd("u1", h, step, 0, lambda step=step: self.ref(2, 0, h, (1 - step) // 2))

    def u2s(self, h, step):
        got = self.rcv("u1", h, step, 0)
        mine = self.ref(step, 0, h, (1 - step) // 2)
        mine[...] = (mine[...].astype(F32) + got[...].astype(F32)).astype(BF)
        self.snd("u2", h, step, 0, lambda: self.ref(step, 0, h, "all"))

    def last(self, h):
        one, two = self.rcv("u2", h, 1, 0), self.rcv("u2", h, -1, 0)
        mine = self.ref(0, 0, h, "all")
        return mine[...].astype(F32) + one[...].astype(F32) + two[...].astype(F32)

    def begin(self):
        for du in (2, -1, 1, 0):
            for h in (0, 1):
                for step in (1, -1):
                    self.v1(h, step, du)

    def middle(self):
        for du in (2, -1, 1, 0):
            for h in (0, 1):
                for step in (1, -1):
                    self.v2(h, step, du)

    def tail_one(self):
        for h in (0, 1):
            self.vsum(h, 2)
            self.u1s(h)

    def tail_two(self):
        for h in (0, 1):
            for step in (1, -1):
                self.vsum(h, step)
                self.u2s(h, step)

    def tail_three(self):
        for h in (0, 1):
            self.vsum(h, 0)


def pick(n, values):
    out = 0
    for j, v in enumerate(values):
        out = out + (n == j).astype(jnp.int32) * v
    return out


def mates_gather(place, links, own, full, tag):
    rows = pl.ds(pl.multiple_of(place.core * 128, 128), 128)
    for r in (2, 1):
        device = place.mate(r)[2]
        links.send((tag, r), lambda device=device: (own, full.at[place.tensor, rows], device))
    full[place.tensor, rows] = own[...]


def mates_gathered(place, links, full, tag):
    rows = pl.ds(pl.multiple_of(place.core * 128, 128), 128)
    others = pl.ds(pl.multiple_of(128 - place.core * 128, 128), 128)
    far, sibling = place.mate(2)[2], place.mate(1)[2]
    links.arrived((tag, 2), full.at[1 - place.tensor, rows], far)
    passed = full.at[1 - place.tensor, rows]
    links.send((tag, 3), lambda: (passed, passed, sibling))
    links.arrived((tag, 1), full.at[place.tensor, others], sibling)
    links.arrived((tag, 3), full.at[1 - place.tensor, others], sibling)


def mates_scatter(place, links, part, rounded, landing, tag):
    others = pl.ds(pl.multiple_of(128 - place.core * 128, 128), 128)
    rounded[:, others] = part[:, others].astype(BF)
    device = place.mate(1)[2]
    links.send((tag, 1), lambda: (rounded.at[:, others], landing.at[pl.ds(0, 2)], device))


def mates_scattered(place, links, part, rounded, landing, tag):
    rows = pl.ds(pl.multiple_of(place.core * 128, 128), 128)
    links.arrived((tag, 1), landing.at[pl.ds(0, 2)], place.mate(1)[2])
    away = part[1 - place.tensor, rows] + landing[1 - place.tensor].astype(F32)
    rounded[1 - place.tensor, rows] = away.astype(BF)
    device = place.mate(2)[2]
    links.send((tag, 2), lambda: (rounded.at[1 - place.tensor, rows], landing.at[2], device))
    total = part[place.tensor, rows] + landing[place.tensor].astype(F32)
    links.arrived((tag, 2), landing.at[2], device)
    return total + landing[2].astype(F32)


def normalize(values):
    centered = values - jnp.mean(values, axis=-1, keepdims=True)
    variance = jnp.mean(centered * centered, axis=-1, keepdims=True)
    scale = lax.rsqrt(variance + EPS)
    return centered * scale, scale


def lane_mask(lower, shape=(ROWS, 128)):
    lane = lax.broadcasted_iota(jnp.int32, shape, 1)
    return lane < 64 if lower else lane >= 64


def turn(values, tab, lower, upper, sign=1.0):
    cosine, plus, minus = tab[0], tab[1], tab[2]
    turned = (
        values * cosine
        + sign * (pltpu.roll(values, 8, 1) * plus + pltpu.roll(values, 120, 1) * minus)
    )
    if lower and upper:
        return turned
    return jnp.where(lane_mask(lower), turned, values)


def weights_kernel(
    qkv, out, fc_in, fc_out, gain, shift, qkv_b, in_b, out_b, mine, theirs, all_small,
    own, buf, raw, turned, small, got_small, send_sems, recv_sems, local,
):
    place = Place()
    links = Links(send_sems, recv_sems)
    core = place.core
    loads = [pltpu.make_async_copy(qkv, raw, local.at[0])]
    for i, block in enumerate((1, 0, 2)):
        rows = pl.ds(pl.multiple_of(core * 192 + block * 64, 64), 64)
        loads.append(pltpu.make_async_copy(out.at[rows], own.at[pl.ds(O0 + i * 64, 64)], local.at[1 + i]))
    half = pl.ds(pl.multiple_of(core * 768, 768), 768)
    loads.append(pltpu.make_async_copy(fc_in.at[:, half], own.at[pl.ds(I0, 768)], local.at[4]))
    loads.append(pltpu.make_async_copy(fc_out.at[half], own.at[pl.ds(U0, 768)], local.at[5]))
    for load in loads:
        load.start()
    place.greet(partner=True)
    small[...] = jnp.zeros_like(small)
    small[0:2] = gain[...].astype(F32)
    small[2:4] = shift[...].astype(F32)
    bias = qkv_b[...].astype(F32)
    bias = jnp.where(core == 0, bias[:, 0:192], bias[:, 192:384])
    pieces = [bias[j : j + 1, h * 64 : h * 64 + 64] for j, h in BLOCKS]
    small[4:5, 0:576] = jnp.concatenate(pieces, axis=1)
    wide = in_b[...].astype(F32)
    small[5:6] = jnp.where(core == 0, wide[:, 0:768], wide[:, 768:1536])
    small[6:7, 0:384] = out_b[...].astype(F32)
    rounded = small[...].astype(BF)
    all_small[place.pipe] = rounded
    loads[0].wait()
    for j in range(3):
        turned[...] = raw[j].T
        for i, (k, h) in enumerate(BLOCKS):
            if k == j:
                own[i * 64 : i * 64 + 64, :] = turned[pl.ds(pl.multiple_of(core * 192 + h * 64, 64), 64), :]
    for load in loads[1:]:
        load.wait()
    device = place.partner()
    for i, (base, rows) in enumerate(PARTS):
        src = own.at[pl.ds(pl.multiple_of(place.chip * PIECE + base, 16), rows)]
        dst = buf.at[place.chip, pl.ds(base, rows)]
        links.send(("slab", i), lambda src=src, dst=dst: (src, dst, device))
    got_small[0] = rounded
    links.send("small", lambda: (got_small.at[0], got_small.at[1], device))
    keep = pltpu.make_async_copy(own, mine, local.at[6])
    keep.start()

    def piece(i):
        links.arrived(("slab", i), buf.at[place.chip, pl.ds(*PARTS[i])], device)

    gather_parts([Gather(place, links, buf, part_view(i), i) for i in range(2)], piece)
    store = pltpu.make_async_copy(buf, theirs, local.at[7])
    store.start()
    links.arrived("small", got_small.at[1], device)
    all_small[1 - place.pipe] = got_small[1]
    keep.wait()
    store.wait()
    links.finish()


def load_layer(l, place, mine, theirs, w, sem):
    pl.when(place.pipe == l)(lambda: pltpu.make_async_copy(mine, w, sem).start())
    pl.when(place.pipe != l)(lambda: pltpu.make_async_copy(theirs, w, sem).start())
    return pltpu.make_async_copy(mine, w, sem)


ORDER_F = ((0, -1), (0, 1), (-1, 0), (1, 0), (-1, -1), (-1, 1), (1, -1), (1, 1), (0, 2), (2, 0), (-1, 2), (2, -1), (1, 2), (2, 1), (2, 2))
ORDER_B = ((2, 2), (0, 2), (2, 0), (-1, 2), (1, 2), (2, -1), (2, 1), (-1, -1), (-1, 1), (1, -1), (1, 1), (0, -1), (0, 1), (-1, 0), (1, 0))


def forward_part(
    l, place, links, load, x_ref, small, tab, y_ref, xg, kvb, q_o, ot_o, lse_o, inner_o,
    w, acc, top, total, part, rounded, landing,
):
    mates_gather(place, links, x_ref, xg, ("x", l))
    vectors = small[l].astype(F32)
    mates_gathered(place, links, xg, ("x", l))
    x = jnp.concatenate([xg[0], xg[1]], axis=1).astype(F32)
    normed, _ = normalize(x)
    first = (normed * vectors[0:1] + vectors[2:3]).astype(BF)
    second = (normed * vectors[1:2] + vectors[3:4]).astype(BF)
    load.wait()
    kv = dot(first, w[KV0:Q0, :], NT) + vectors[4:5, 0:384]
    for h in range(3):
        tile = kv[:, h * 128 : h * 128 + 128]
        kvb[place.chip, :, h * 128 : h * 128 + 128] = turn(tile, tab, h != 1, h == 1).astype(BF)
    gather = Gather(place, links, kvb, kv_view, ("kv", l))
    gather.begin()
    low, high = lane_mask(True), lane_mask(False)
    qa = dot(first, w[Q0 : Q0 + 128, :], NT) + vectors[4:5, 384:512]
    qb = dot(first, w[Q0 + 64 : Q0 + 192, :], NT)
    qa = (turn(qa, tab, True, True)).astype(BF) * HD**-0.5
    qb = pltpu.roll(qb, 64, 1) + vectors[4:5, 512:640]
    qb = (turn(qb, tab, True, False)).astype(BF) * HD**-0.5
    zero = jnp.zeros((ROWS, 128), BF)
    q_o[0] = jnp.where(low, qa, zero)
    q_o[1] = jnp.where(high, qa, zero)
    q_o[2] = jnp.where(low, qb, zero)
    gather.first()
    gather.own_line()
    inner = dot(second, w[I0:U0, :]) + vectors[5:6]
    inner_o[...] = inner
    act = (inner * (0.5 * (1.0 + lax.erf(inner * (2.0**-0.5))))).astype(BF)
    gather.second()
    branch = dot(act, w[U0:SLAB, :])
    part[0] = branch[:, 0:384]
    part[1] = branch[:, 384:768]

    def scores(kk, h):
        keys = kvb[kk, :, h * 128 : h * 128 + 128]
        return keys, dot(keys, q_o[h], NT)

    causal = lax.broadcasted_iota(jnp.int32, (ROWS, ROWS), 0) <= lax.broadcasted_iota(
        jnp.int32, (ROWS, ROWS), 1
    )
    for h in range(3):
        keys, s = scores(place.chip, h)
        s = jnp.where(causal, s, -1e30)
        m = jnp.max(s, axis=0, keepdims=True)
        p = jnp.exp(s - m)
        top[h] = m
        total[h] = jnp.sum(p, axis=0, keepdims=True)
        acc[h] = dot(keys, p.astype(BF), TN)

    def step(n, carry):
        for j, action in (
            (0, lambda: gather.third(0)),
            (2, lambda: gather.third(-1)),
            (4, lambda: gather.third(1)),
            (6, lambda: gather.third(2)),
            (8, lambda: gather.fourth(0)),
            (10, lambda: gather.fourth(-1)),
            (12, lambda: gather.fourth(1)),
            (14, lambda: gather.fourth(2)),
        ):
            pl.when(n == j)(action)
        kk = place.slot(pick(n, [o[0] for o in ORDER_F]), pick(n, [o[1] for o in ORDER_F]))

        @pl.when(kk < place.chip)
        def _():
            for h in range(3):
                keys, s = scores(kk, h)
                old = top[h]
                m = jnp.maximum(old, jnp.max(s, axis=0, keepdims=True))
                p = jnp.exp(s - m)
                fade = jnp.exp(old - m)
                top[h] = m
                total[h] = total[h] * fade + jnp.sum(p, axis=0, keepdims=True)
                acc[h] = acc[h] * fade + dot(keys, p.astype(BF), TN)

        return carry

    lax.fori_loop(0, 15, step, 0)
    heads = []
    for h in range(3):
        rows = slice(0, 64) if h == 1 else slice(64, 128)
        heads.append(acc[h, rows, :] / total[h])
        lse_o[h : h + 1, :] = top[h] + jnp.log(total[h])
    attn = jnp.concatenate([heads[1], heads[0], heads[2]], axis=0)
    ot_o[...] = attn
    branch = dot(attn.astype(BF), w[O0:I0, :], TN)
    part[0] = part[0] + branch[:, 0:384]
    part[1] = part[1] + branch[:, 384:768]
    mates_scatter(place, links, part, rounded, landing, ("y", l))
    y = mates_scattered(place, links, part, rounded, landing, ("y", l))
    y_ref[...] = (y + x_ref[...].astype(F32) + vectors[6:7, 0:384]).astype(BF)


def backward_part(
    l, place, links, g_ref, xg, small, tab, tabt, kvb, q, ot, lse, inner, gx_ref, wg, sg,
    w, gg, dkv, dqt, do, first, second, act, slope, part, rounded, landing, r1, r2, u1, u2,
    upper=None, piece=None, ready=lambda: None,
):
    mates_gather(place, links, g_ref, gg, ("g", l))
    if upper is not None:
        upper.begin()
    vectors = small[l].astype(F32)
    x = jnp.concatenate([xg[0], xg[1]], axis=1).astype(F32)
    normed, scale = normalize(x)
    first[...] = (normed * vectors[0:1] + vectors[2:3]).astype(BF)
    second[...] = (normed * vectors[1:2] + vectors[3:4]).astype(BF)
    value = inner[...]
    cdf = 0.5 * (1.0 + lax.erf(value * (2.0**-0.5)))
    act[...] = (value * cdf).astype(BF)
    slope[...] = cdf + value * jnp.exp(-0.5 * value * value) * 0.3989422804014327
    mates_gathered(place, links, gg, ("g", l))
    g = jnp.concatenate([gg[0], gg[1]], axis=1)
    low, high = lane_mask(True), lane_mask(False)
    zero = jnp.zeros((ROWS, 128), BF)
    da = dot(g, w[O0 : O0 + 128, :], NT).astype(BF)
    db = dot(g, w[O0 + 64 : O0 + 192, :], NT).astype(BF)
    do[0] = jnp.where(high, da, zero)
    do[1] = jnp.where(low, da, zero)
    do[2] = jnp.where(high, db, zero)
    dot_t = dot(w[O0:I0, :], g, NT).astype(BF).astype(F32) * ot[...]
    delta = [
        jnp.sum(dot_t[s : s + 64], axis=0, keepdims=True) for s in (64, 0, 128)
    ]
    if upper is not None:
        upper.middle()
    dqt[...] = jnp.zeros_like(dqt)
    scatter = Scatter(place, links, dkv, kv_view, r1, r2, u1, u2, ("d", l))

    def chunk(kk, mask):
        for h in range(3):
            keys = kvb[kk, :, h * 128 : h * 128 + 128]
            p = jnp.exp(dot(keys, q[h], NT) - lse[h : h + 1, :])
            if mask is not None:
                p = jnp.where(mask, p, 0.0)
            dp = dot(keys, do[h], NT)
            ds = (p * (dp - delta[h])).astype(BF)
            dkv[kk, :, h * 128 : h * 128 + 128] = (dot(ds, q[h]) + dot(p.astype(BF), do[h])).astype(BF)
            dqt[h] = dqt[h] + dot(keys, ds, TN)

    def events(j):
        a, b = ORDER_B[j]
        if b == 2:
            for s in (1, -1):
                scatter.v1(0, s, a)
        if a == 2:
            for s in (1, -1):
                scatter.v1(1, s, b)
        if j == 7:
            for s in (1, -1):
                scatter.v2(0, s, 2)
                scatter.v2(1, s, 2)
        if j >= 7:
            if b in (1, -1):
                scatter.v2(0, b, a)
            if a in (1, -1):
                scatter.v2(1, a, b)

    def step(n, carry):
        kk = place.slot(pick(n, [o[0] for o in ORDER_B]), pick(n, [o[1] for o in ORDER_B]))

        @pl.when(kk < place.chip)
        def _():
            chunk(kk, None)

        @pl.when(kk > place.chip)
        def _():
            dkv[kk] = jnp.zeros((ROWS, 384), BF)

        for j in range(15):
            pl.when(n == j)(functools.partial(events, j))
        return carry

    lax.fori_loop(0, 15, step, 0)
    chunk(
        place.chip,
        lax.broadcasted_iota(jnp.int32, (ROWS, ROWS), 0)
        <= lax.broadcasted_iota(jnp.int32, (ROWS, ROWS), 1),
    )
    g = jnp.concatenate([gg[0], gg[1]], axis=1)
    grad_inner = (dot(g, w[U0:SLAB, :], NT) * slope[...]).astype(BF)
    wg[U0:SLAB, :] = dot(act[...], g, TN).astype(BF)
    if upper is not None:
        upper.tail_one()
    scatter.tail_one()
    wg[I0:U0, :] = dot(second[...], grad_inner, TN).astype(BF)
    if upper is not None:
        upper.tail_two()
    scatter.tail_two()
    grad_second = dot(grad_inner, w[I0:U0, :], NT)
    wg[O0:I0, :] = dot(ot[...].astype(BF), g).astype(BF)
    scatter.tail_three()
    if upper is not None:
        upper.tail_three()
    sg[0:1, :] = jnp.sum(grad_second * normed, axis=0, keepdims=True)
    sg[1:2, :] = jnp.sum(grad_second, axis=0, keepdims=True)
    sg[2:3, :] = jnp.sum(grad_inner.astype(F32), axis=0, keepdims=True)
    sg[3:4, :] = jnp.sum(g.astype(F32), axis=0, keepdims=True)
    sg[6:8, :] = jnp.zeros((2, D), F32)
    rows = []
    for h in range(3):
        base = 64 if h == 1 else 0
        dq = dqt[h, base : base + 64, :] * HD**-0.5
        a, b = dq[0:8], dq[8:16]
        rows += [a * tabt[0] + b * tabt[1], b * tabt[0] - a * tabt[1], dq[16:64]]
    dq = jnp.concatenate(rows, axis=0).astype(BF)
    wg[Q0:O0, :] = dot(dq, first[...]).astype(BF)
    grad_first = dot(dq, w[Q0:O0, :], TN)
    q_sums = dot(jnp.ones((8, ROWS), BF), dq, NT)
    pre = jnp.concatenate([scatter.last(0), scatter.last(1)], axis=0)
    tiles = [
        turn(pre[:, h * 128 : h * 128 + 128], tab, h != 1, h == 1, -1.0).astype(BF)
        for h in range(3)
    ]
    pre = jnp.concatenate(tiles, axis=1)
    wg[KV0:Q0, :] = dot(pre, first[...], TN).astype(BF)
    ready()
    grad_first = grad_first + dot(pre, w[KV0:Q0, :])
    sg[4:5, :] = jnp.sum(grad_first * normed, axis=0, keepdims=True)
    sg[5:6, :] = jnp.sum(grad_first, axis=0, keepdims=True)
    sg[6:7, 0:384] = jnp.sum(pre.astype(F32), axis=0, keepdims=True)
    sg[7:8, 0:192] = q_sums[0:1, :]
    grad_norm = grad_first * vectors[0:1] + grad_second * vectors[1:2]
    grad_x = scale * (
        grad_norm
        - jnp.mean(grad_norm, axis=-1, keepdims=True)
        - normed * jnp.mean(grad_norm * normed, axis=-1, keepdims=True)
    )
    part[0] = grad_x[:, 0:384]
    part[1] = grad_x[:, 384:768]
    mates_scatter(place, links, part, rounded, landing, ("gx", l))
    if upper is not None:
        for h in (0, 1):
            piece[:, h * 384 : h * 384 + 384] = upper.last(h)
    grad = mates_scattered(place, links, part, rounded, landing, ("gx", l))
    gx_ref[...] = (grad + g_ref[...].astype(F32)).astype(BF)


class Rows:
    def __init__(self, ref):
        self.ref = ref

    def __setitem__(self, index, value):
        start, stop = index[0].start, index[0].stop
        for row in range(start, stop, 48):
            self.ref[row // PIECE, row % PIECE : row % PIECE + 48, :] = value[row - start : row - start + 48]


def layers_kernel(
    x_ref, g_ref, slab, slab2, small, tab, tabt, edge, out, out_small,
    w, middle, xg, kvb, q, ot, lse, inner, acc, top, total, part, rounded, landing,
    g_mid, gg, dkv, do, first, second, act, slope, r1, r2, u1, u2, wg1, a1, a2, b1, b2,
    ends, wg0, sg0, sg1, piece1, c1, c2, d1, d2, buf, piece, got, sm, along_x, along_z, across,
    beside, send_sems, recv_sems, local,
):
    place = Place()
    links = Links(send_sems, recv_sems)
    y_ref, gx_ref = ends.at[0], ends.at[1]
    lower = Scatter(place, links, wg0, slab_view, c1, c2, d1, d2, "w0")
    loads = [load_layer(l, place, slab, slab2, w.at[l], local.at[l]) for l in (0, 1)]
    place.greet(mates=(1, 2, 3), partner=True, far=True)
    for l, (entry, exit_ref) in enumerate(((x_ref, middle), (middle, y_ref))):
        forward_part(
            l, place, links, loads[l], entry, small, tab, exit_ref, xg.at[l], kvb.at[l], q.at[l],
            ot.at[l], lse.at[l], inner.at[l], w.at[l], acc, top, total, part, rounded.at[l],
            landing.at[l],
        )
    for l, entry, exit_ref, wg, sg in ((1, g_ref, g_mid, wg1, sg1), (0, g_mid, gx_ref, wg0, sg0)):
        upper = Scatter(place, links, wg1, slab_view, a1, a2, b1, b2, "w") if l == 0 else None
        backward_part(
            l, place, links, entry, xg.at[l], small, tab, tabt, kvb.at[l], q.at[l], ot.at[l],
            lse.at[l], inner.at[l], exit_ref, Rows(wg), sg, w.at[l], gg.at[l], dkv.at[l], acc, do,
            first, second, act, slope, part, rounded.at[2 + l], landing.at[2 + l],
            r1.at[l], r2.at[l], u1.at[l], u2.at[l], upper, piece1,
            lower.begin if l == 0 else lambda: None,
        )
    lower_pipe = place.pipe == 0
    ends[2] = jnp.where(lower_pipe, ends[0], ends[1])
    edge[place.pipe] = jnp.where(lower_pipe, ends[1], ends[0])
    links.send("edge", lambda: (ends.at[2], ends.at[3], place.partner()))
    grads_part(
        place, links, lower, sg0, sg1, piece1, out, out_small, buf, piece, got,
        sm, along_x, along_z, across, beside, local,
    )
    links.arrived("edge", ends.at[3], place.partner())
    edge[1 - place.pipe] = ends[3]
    links.finish()


def grads_part(
    place, links, scatter, sg0, sg1, piece1, out, out_small, buf, piece, got,
    sm, along_x, along_z, across, beside, local,
):
    sm[0, 0] = sg0[...]
    sm[0, 1] = sg1[...]
    for d in (1, 2, 3):
        links.send(("sx", d), lambda d=d: (sm.at[0], along_x.at[d - 1], place.at(d, 0)))

    def small_z():
        total = sm[0]
        for d in (1, 2, 3):
            links.arrived(("sx", d), along_x.at[d - 1], place.at(d, 0))
            total = total + along_x[d - 1]
        sm[1] = total
        for d in (1, 2, 3):
            links.send(("sz", d), lambda d=d: (sm.at[1], along_z.at[d - 1], place.at(0, d)))

    def small_pipe():
        total = sm[1]
        for d in (1, 2, 3):
            links.arrived(("sz", d), along_z.at[d - 1], place.at(0, d))
            total = total + along_z[d - 1]
        sm[2] = total
        links.send("sp", lambda: (sm.at[2, 1 - place.pipe], across, place.partner()))

    def small_mates():
        links.arrived("sp", across, place.partner())
        sm[3, 0] = sm[2, place.pipe] + across[...]
        for r in (1, 2, 3):
            links.send(("sm", r), lambda r=r: (sm.at[3, 0], beside.at[r - 1], place.mate(r)[2]))

    def small_last():
        total = sm[3, 0]
        for r in (1, 2, 3):
            links.arrived(("sm", r), beside.at[r - 1], place.mate(r)[2])
            total = total + beside[r - 1]
        row = lax.broadcasted_iota(jnp.int32, (8, D), 0)
        norm = (row < 2) | ((row >= 4) & (row < 6))
        out_small[place.core] = jnp.where(norm, total, sm[3, 0])
        out_small[1 - place.core] = jnp.where(norm, total, beside[0])

    small_z()
    scatter.middle()
    small_pipe()
    scatter.tail_one()
    scatter.tail_two()
    scatter.tail_three()
    small_mates()
    device = place.partner()
    lower_pipe = place.pipe == 0
    for h in (0, 1):
        lanes = pl.ds(h * 384, 384)
        zero, one = scatter.last(h), piece1[:, lanes]
        piece[:, lanes] = jnp.where(lower_pipe, zero, one)
        got[0, :, lanes] = jnp.where(lower_pipe, one, zero).astype(BF)
    for i, (base, rows) in enumerate(PARTS):
        span = pl.ds(base, rows)
        links.send(("piece", i), lambda span=span: (got.at[0, span], got.at[1, span], device))

    def whole(i):
        span = pl.ds(*PARTS[i])
        links.arrived(("piece", i), got.at[1, span], device)
        buf[place.core, place.chip, span] = (piece[span] + got[1, span].astype(F32)).astype(BF)

    sibling = place.mate(1)[2]

    def pass_on(a, b):
        ref = lambda: buf.at[place.core, place.slot(a, b)]
        links.send(("core", a, b), lambda: (ref(), ref(), sibling))

    parts = [Gather(place, links, buf.at[place.core], part_view(i), i) for i in range(2)]
    gather_parts(parts, whole, pass_on)
    keep = pltpu.make_async_copy(buf.at[place.core], out.at[place.core], local.at[2])
    keep.start()
    small_last()
    for a, b in ((0, 0), *ORDER_F):
        links.arrived(("core", a, b), buf.at[1 - place.core, place.slot(a, b)], sibling)
    rest = pltpu.make_async_copy(buf.at[1 - place.core], out.at[1 - place.core], local.at[3])
    rest.start()
    keep.wait()
    rest.wait()


VMEM = pl.BlockSpec(memory_space=pltpu.VMEM)
ANY = pl.BlockSpec(memory_space=pl.ANY)


def sems(n, m):
    return [pltpu.SemaphoreType.DMA((n,)), pltpu.SemaphoreType.DMA((n,)), pltpu.SemaphoreType.DMA((m,))]


def shape(dims, kind=BF):
    return jax.ShapeDtypeStruct(dims, kind)


def params(i):
    return pltpu.CompilerParams(collective_id=i, has_side_effects=True, vmem_limit_bytes=62 * 2**20)


def share_weights(*args):
    return pl.pallas_call(
        weights_kernel,
        name="share_weights",
        out_shape=(shape((SLAB, D)), shape((CHIPS, PIECE, D)), shape((2, 16, D))),
        in_specs=[ANY, ANY, ANY, ANY, VMEM, VMEM, VMEM, VMEM, VMEM],
        out_specs=(ANY, ANY, VMEM),
        scratch_shapes=[
            pltpu.VMEM((SLAB, D), BF),
            pltpu.VMEM((CHIPS, PIECE, D), BF),
            pltpu.VMEM((3, D, 384), BF),
            pltpu.VMEM((384, D), BF),
            pltpu.VMEM((16, D), F32),
            pltpu.VMEM((2, 16, D), BF),
            *sems(96, 8),
        ],
        compiler_params=params(0),
    )(*args)


def landing_shapes(rows, part, lead=()):
    return [
        pltpu.VMEM((*lead, 2, 2, 4, part, 384), BF),
        pltpu.VMEM((*lead, 2, 2, 4, rows, 384), BF),
        pltpu.VMEM((*lead, 2, 2, part, 384), BF),
        pltpu.VMEM((*lead, 2, 2, rows, 384), BF),
    ]


def layers(*args):
    def pair(dims, kind=BF, n=2):
        return pltpu.VMEM((n, *dims), kind)

    return pl.pallas_call(
        layers_kernel,
        name="layers",
        out_shape=(shape((2, 128, 384)), shape((2, CHIPS, PIECE, D)), shape((2, 8, D), F32)),
        in_specs=[VMEM, VMEM, ANY, ANY, VMEM, VMEM, VMEM],
        out_specs=(VMEM, ANY, VMEM),
        scratch_shapes=[
            pair((SLAB, D)),
            pltpu.VMEM((128, 384), BF),
            pair((2, ROWS, 384)),
            pair((CHIPS, ROWS, 384)),
            pair((3, ROWS, 128)),
            pair((192, ROWS), F32),
            pair((8, ROWS), F32),
            pair((ROWS, D), F32),
            pltpu.VMEM((3, 128, ROWS), F32),
            pltpu.VMEM((3, 1, ROWS), F32),
            pltpu.VMEM((3, 1, ROWS), F32),
            pltpu.VMEM((2, ROWS, 384), F32),
            pair((2, ROWS, 384), n=4),
            pair((3, 128, 384), n=4),
            pltpu.VMEM((128, 384), BF),
            pair((2, ROWS, 384)),
            pair((CHIPS, ROWS, 384)),
            pltpu.VMEM((3, ROWS, 128), BF),
            pltpu.VMEM((ROWS, D), BF),
            pltpu.VMEM((ROWS, D), BF),
            pltpu.VMEM((ROWS, D), BF),
            pltpu.VMEM((ROWS, D), F32),
            *landing_shapes(128, 64, (2,)),
            pltpu.VMEM((CHIPS, PIECE, D), BF),
            *landing_shapes(PIECE, 80),
            pltpu.VMEM((4, 128, 384), BF),
            pltpu.VMEM((CHIPS, PIECE, D), BF),
            pltpu.VMEM((8, D), F32),
            pltpu.VMEM((8, D), F32),
            pltpu.VMEM((PIECE, D), F32),
            *landing_shapes(PIECE, 80),
            pltpu.VMEM((2, CHIPS, PIECE, D), BF),
            pltpu.VMEM((PIECE, D), F32),
            pltpu.VMEM((2, PIECE, D), BF),
            pltpu.VMEM((4, 2, 8, D), F32),
            pltpu.VMEM((3, 2, 8, D), F32),
            pltpu.VMEM((3, 2, 8, D), F32),
            pltpu.VMEM((8, D), F32),
            pltpu.VMEM((3, 8, D), F32),
            *sems(376, 4),
        ],
        compiler_params=params(1),
    )(*args)


def finish_kernel(
    whole, small, g_qkv, g_out, g_in, g_down, g_gain, g_shift, g_qkv_b, g_out_b, g_in_b,
    held, qkv, out, wide, down, local,
):
    regions = ((U0, SLAB), (I0, U0), (O0, I0), (KV0, O0))
    loads = []
    for i, (lo, hi) in enumerate(regions):
        for c in (0, 1):
            rows = pl.ds(lo, hi - lo)
            load = pltpu.make_async_copy(whole.at[c, rows], held.at[c, rows], local.at[2 * i + c])
            load.start()
            loads.append(load)
    tensor = lax.axis_index("tensor")
    rows = [small[0], small[1]]

    def features(row):
        return jnp.where(tensor == 0, row[:, 0:384], row[:, 384:768])

    g_gain[0:1] = features(rows[0][4:5])
    g_gain[1:2] = features(rows[0][0:1])
    g_shift[0:1] = features(rows[0][5:6])
    g_shift[1:2] = features(rows[0][1:2])
    g_out_b[...] = features(rows[0][3:4])
    g_in_b[...] = jnp.concatenate([rows[0][2:3], rows[1][2:3]], axis=1)
    for j in range(3):
        pieces = []
        for c in (0, 1):
            for i in [BLOCKS.index((j, h)) for h in range(3)]:
                row, at = (6, i) if i < 6 else (7, i - 6)
                pieces.append(rows[c][row : row + 1, at * 64 : at * 64 + 64])
        g_qkv_b[j : j + 1] = jnp.concatenate(pieces, axis=1)
    stores = []

    def store(i, src, dst):
        copy = pltpu.make_async_copy(src, dst, local.at[8 + i])
        copy.start()
        stores.append(copy)

    for c in (0, 1):
        loads[c].wait()
        down[c * 768 : c * 768 + 768] = held[c, U0:SLAB].astype(F32)
        store(c, down.at[pl.ds(c * 768, 768)], g_down.at[pl.ds(c * 768, 768)])
    for c in (0, 1):
        loads[2 + c].wait()
        wide[:, c * 768 : c * 768 + 768] = held[c, I0:U0].astype(F32)
    store(2, wide, g_in)
    for c in (0, 1):
        loads[4 + c].wait()
        for i, block in enumerate((1, 0, 2)):
            start = c * 192 + block * 64
            out[start : start + 64] = held[c, O0 + i * 64 : O0 + i * 64 + 64].astype(F32)
    store(3, out, g_out)
    for c in (0, 1):
        loads[6 + c].wait()
    for j in range(3):
        pieces = []
        for c in (0, 1):
            for i in [BLOCKS.index((j, h)) for h in range(3)]:
                pieces.append(held[c, i * 64 : i * 64 + 64])
        qkv[j] = jnp.concatenate(pieces, axis=0).astype(F32).T
        store(4 + j, qkv.at[j], g_qkv.at[j])
    for copy in stores:
        copy.wait()


def finish(whole, small):
    return pl.pallas_call(
        finish_kernel,
        name="finish",
        out_shape=(
            shape((3, D, 384), F32),
            shape((384, D), F32),
            shape((D, 1536), F32),
            shape((1536, D), F32),
            shape((2, 384), F32),
            shape((2, 384), F32),
            shape((3, 384), F32),
            shape((1, 384), F32),
            shape((1, 1536), F32),
        ),
        in_specs=[ANY, VMEM],
        out_specs=(ANY, ANY, ANY, ANY, VMEM, VMEM, VMEM, VMEM, VMEM),
        scratch_shapes=[
            pltpu.VMEM((2, SLAB, D), BF),
            pltpu.VMEM((3, D, 384), F32),
            pltpu.VMEM((384, D), F32),
            pltpu.VMEM((D, 1536), F32),
            pltpu.VMEM((1536, D), F32),
            pltpu.SemaphoreType.DMA((16,)),
        ],
        compiler_params=pltpu.CompilerParams(vmem_limit_bytes=56 * 2**20),
    )(whole, small)


def rope_tables(chip):
    half = HD // 8
    freqs = 10000.0 ** (-2.0 * jnp.arange(half, dtype=F32) / (2 * half))
    positions = chip * ROWS + jnp.arange(ROWS, dtype=jnp.int32)
    angles = positions.astype(F32)[:, None] * freqs[None, :]
    cosine, sine = jnp.cos(angles), jnp.sin(angles)
    none = jnp.zeros((ROWS, half), F32)
    rest = jnp.zeros((ROWS, HD - 2 * half), F32)
    tiles = [
        jnp.concatenate([cosine, cosine, rest + 1.0], axis=1),
        jnp.concatenate([none, sine, rest], axis=1),
        jnp.concatenate([-sine, none, rest], axis=1),
    ]
    tab = jnp.stack([jnp.concatenate([tile, tile], axis=1) for tile in tiles])
    return tab, jnp.stack([cosine.T, sine.T])


def body(
    inputs, cotangent, ln_gain, ln_bias, qkv_weight, qkv_bias, out_weight, out_bias,
    fc_in_weight, fc_in_bias, fc_out_weight,
):
    pipe = lax.axis_index("pipe")
    ctx = lax.axis_index("ctx")
    tab, tabt = rope_tables(ctx // 2)
    mine, theirs, smalls = share_weights(
        qkv_weight[0], out_weight[0], fc_in_weight[0], fc_out_weight[0], ln_gain[0], ln_bias[0],
        qkv_bias[0], fc_in_bias, out_bias,
    )
    slabs = mine, theirs.reshape(SLAB, D)

    x = lax.dynamic_index_in_dim(inputs, pipe, 0, keepdims=False)
    g = lax.dynamic_index_in_dim(cotangent, pipe, 0, keepdims=False)
    edge, whole, sums = layers(x, g, *slabs, smalls, tab, tabt)
    g_qkv, g_out, g_in, g_down, g_gain, g_shift, g_qkv_b, g_out_b, g_in_b = finish(
        whole.reshape(2, SLAB, D), sums
    )
    return (
        edge[None],
        g_gain[None],
        g_shift[None],
        g_qkv[None],
        g_qkv_b[None],
        g_out[None],
        g_out_b,
        g_in[None],
        g_in_b,
        g_down[None],
    )


def solution(mesh):
    return jax.shard_map(
        body,
        mesh=mesh,
        in_specs=(
            P(None, "ctx", "tensor"),
            P(None, "ctx", "tensor"),
            P("pipe", None, None),
            P("pipe", None, None),
            P("pipe", None, None, "tensor"),
            P("pipe", None, "tensor"),
            P("pipe", "tensor", None),
            P("pipe", "tensor"),
            P("pipe", None, "tensor"),
            P("pipe", "tensor"),
            P("pipe", "tensor", None),
        ),
        out_specs=(
            P("pipe", None, "ctx", "tensor"),
            P("pipe", None, "tensor"),
            P("pipe", None, "tensor"),
            P("pipe", None, None, "tensor"),
            P("pipe", None, "tensor"),
            P("pipe", "tensor", None),
            P("pipe", "tensor"),
            P("pipe", None, "tensor"),
            P("pipe", "tensor"),
            P("pipe", "tensor", None),
        ),
        check_vma=False,
    )
```
